128 devices in a mesh: leaf: 8 (over z, x_hi), grid: 16 (over y, x_lo, core).
Axes of the slice: x: 4 (x_hi: 2, x_lo: 2; x = x_hi * 2 + x_lo), y: 4, z: 4, core: 2. Of those that a mesh axis runs over, the one named last changes fastest.
Arguments:
- root_inverse: float32 [4096, 4096], P('grid', 'leaf'), may hold values from -1 to 12, as said below
- middle_inverse: float32 [2048, 4096], P('grid', 'leaf'), may hold values from -1 to 12, as said below
- middle_panel: float32 [4096, 4096], P('grid', 'leaf'), may hold values from -0.1875 to 0.1875
- lower_root: float32 [4096, 8192], P('grid', 'leaf'), may hold values from -0.1875 to 0.1875
- lower_middle: float32 [2048, 8192], P(None, 'leaf'), may hold values from -0.25 to 0.25
- block_pattern: int32 [4, 32], replicated, may hold values 0 or 1
- lower_diagonal: float32 [8192], P('leaf'), may hold values from 1.5 to 6
Outputs:
- middle_cross: float32 [4096, 4096], P('grid', 'leaf')
- middle_variance: float32 [4096], P('leaf')
- lower_cross: float32 [4096, 8192], P('grid', 'leaf')
- lower_parent: float32 [2048, 8192], P('grid', 'leaf')
- lower_variance: float32 [8192], P('leaf')
The draws below stay inside these ranges and needn't reach their ends.
Inputs may be any that keep to these rules, and one draw needn't show every extreme that they name: `root_inverse`: symmetric; its diagonal entries lie between 1.5 and 12. `middle_inverse`: each front's 2048 x 2048 block is symmetric; its diagonal entries lie between 1.5 and 12.
All inputs are finite; a program needn't handle non-finite values.
Results may differ from the reference program's by a relative error of at most 0.0001.
Values sent between devices are 32-bit elements; how exact they have to be, the bound alone decides.
A program may use at most 128 MiB of HBM per device.

```python
import math
import jax
import jax.numpy as jnp
from jax import lax

S0 = 4096
S1 = 2048
S2 = 2048
BLK = 128


def symmetric_block(raw, factor, size):
    rise = 1.0 + 3.0 * jnp.arange(size, dtype=jnp.float32) / (size - 1)
    spread = (raw + raw.T) * (0.7071 / jnp.sqrt(jnp.float32(size)))
    eye = jnp.eye(size, dtype=jnp.float32)
    return spread * (1.0 - eye) + eye * (rise * factor)[None, :]


def draw_root_inverse(key, part):
    key = jax.random.fold_in(key, 1)
    first, second = jax.random.split(key)
    raw = jnp.clip(jax.random.normal(first, (S0, S0), jnp.float32), -5.0, 5.0)
    factor = jnp.exp(jax.random.uniform(second, (S0,), jnp.float32, jnp.log(1.5), jnp.log(3.0)))
    return symmetric_block(raw, factor, S0)


def draw_middle_inverse(key, part):
    key = jax.random.fold_in(key, 2)
    blocks = []
    for front in range(2):
        first, second = jax.random.split(jax.random.fold_in(key, 20 + front))
        raw = jnp.clip(jax.random.normal(first, (S1, S1), jnp.float32), -5.0, 5.0)
        factor = jnp.exp(jax.random.uniform(second, (S1,), jnp.float32, jnp.log(1.5), jnp.log(3.0)))
        blocks.append(symmetric_block(raw, factor, S1))
    return jnp.concatenate(blocks, axis=1)


def place_ends(result, own_key, smallest, high):
    dims = result.shape
    spot = [jax.random.randint(jax.random.fold_in(own_key, axis), (), 0, dims[axis]) for axis in range(len(dims))]
    result = result.at[tuple(spot)].set(smallest)
    longest = dims.index(max(dims))
    spot[longest] = (spot[longest] + 1) % dims[longest]
    return result.at[tuple(spot)].set(high)


def levels(stream_key, dims, cuts, low, top_value):
    def one(axis_at, shards_of):
        heights = jax.random.uniform(jax.random.fold_in(jax.random.fold_in(stream_key, 6), axis_at), (shards_of,), jnp.float32, low / len(cuts), top_value / len(cuts))
        return jnp.repeat(jnp.exp(heights), dims[axis_at] // shards_of).reshape((-1,) + (1,) * (len(dims) - axis_at - 1))

    factor_of = one(*cuts[0])
    for cut in cuts[1:]:
        factor_of = factor_of * one(*cut)
    return factor_of


def normal_values(own_key, dims, deviation, limit, pieces=(), kind=jnp.bfloat16):
    entries = deviation * jax.random.normal(own_key, dims, jnp.float32)
    if pieces:
        entries = entries * levels(own_key, dims, pieces, -0.22, 0.18)
    return jnp.clip(entries, -limit, limit).astype(kind)


def setup_inputs(seed: int = 0) -> dict:
    streams_of = jax.random.split(jax.random.key(seed), 8)
    return {
        "root_inverse": draw_root_inverse(jax.random.fold_in(streams_of[7], 71), 0),
        "middle_inverse": draw_middle_inverse(jax.random.fold_in(streams_of[7], 71), 0),
        "middle_panel": normal_values(streams_of[2], (S0, 2 * S1), (S0 // 4) ** -0.5, 0.1875, ((0, 16), (1, 8)), jnp.float32),
        "lower_root": normal_values(streams_of[3], (S0, 4 * S2), (S0 // 4) ** -0.5, 0.1875, ((0, 16), (1, 8)), jnp.float32),
        "lower_middle": normal_values(streams_of[4], (S1, 4 * S2), (S1 // 4) ** -0.5, 0.25, ((1, 8),), jnp.float32),
        "block_pattern": place_ends((jax.random.randint(streams_of[5], (4, S0 // BLK), 0, 3) < 2).astype(jnp.int32), jax.random.fold_in(streams_of[5], 1), 0, 1),
        "lower_diagonal": jnp.clip(jnp.exp(math.log(6.0) - 1.3862944 * jax.random.uniform(streams_of[6], (4 * S2,), jnp.float32) ** levels(streams_of[6], (4 * S2,), ((0, 8),), -0.2, 0.2)), 1.5, 6.0),
    }


def reference(root_inverse, middle_inverse, middle_panel, lower_root, lower_middle, block_pattern, lower_diagonal):
    exact = lax.Precision.HIGHEST
    keep = jnp.repeat(block_pattern.astype(jnp.float32), BLK, axis=1)
    first_side = jnp.dot(root_inverse, middle_panel, precision=exact, preferred_element_type=jnp.float32)
    diagonals = []
    for front in range(2):
        diagonals.append(jnp.diagonal(middle_inverse[:, front * S1:(front + 1) * S1]))
    middle_variance = jnp.concatenate(diagonals) + jnp.sum(middle_panel * first_side, axis=0)
    crosses = []
    parents = []
    lowers = []
    for front in range(4):
        parent = front // 2
        columns = slice(front * S2, (front + 1) * S2)
        parent_columns = slice(parent * S1, (parent + 1) * S1)
        lower_panel = lower_root[:, columns] * keep[front][:, None]
        reduced = lower_panel - jnp.dot(middle_panel[:, parent_columns], lower_middle[:, columns], precision=exact, preferred_element_type=jnp.float32)
        root_side = jnp.dot(root_inverse, reduced, precision=exact, preferred_element_type=jnp.float32)
        parent_side = jnp.dot(middle_inverse[:, parent_columns], lower_middle[:, columns], precision=exact, preferred_element_type=jnp.float32)
        parent_side = parent_side - jnp.dot(middle_panel[:, parent_columns].T, root_side, precision=exact, preferred_element_type=jnp.float32)
        lowers.append(lower_diagonal[columns] + jnp.sum(lower_panel * root_side, axis=0) + jnp.sum(lower_middle[:, columns] * parent_side, axis=0))
        crosses.append(root_side)
        parents.append(parent_side)
    lower_cross = -jnp.concatenate(crosses, axis=1)
    lower_parent = -jnp.concatenate(parents, axis=1)
    return (-first_side, middle_variance, lower_cross, lower_parent, jnp.concatenate(lowers))
```

```python
import functools

import jax
import jax.numpy as jnp
from jax import lax
from jax.experimental import pallas as pl
from jax.experimental.pallas import tpu as pltpu
from jax.sharding import PartitionSpec as P

MESH = pl.DeviceIdType.MESH
F32 = jnp.float32
BF16 = jnp.bfloat16
MIB = 2**20


def device(z, a, y, b, c):
    return (z * 2 + a, y * 4 + b * 2 + c)


def flip(v, k):
    if k == 0:
        return v
    if k == 1:
        return v + 1 - 2 * (v % 2)
    if k == 2:
        return (v + 2) % 4
    return 3 - v


def high_low(x):
    high = x.astype(BF16)
    low = (x - high.astype(F32)).astype(BF16)
    return high, low


def kernel(
    s_hbm, minv_hbm, p_hbm, l_hbm, m_hbm, pattern, diag_ref,
    f_out, mid_out, root_out, par_out, low_out,
    s_buf, p_col, red, p_row, m_row, ft, f_part, ft_src, f_recv, r_part, r_recv, q_part, q_recv,
    m_stage, l_own, m_own, mm, red_acc, sums,
    s_split, red_hi, red_lo, b_hi, b_lo, pc_hi, pc_lo, a_tmp, q_tmp,
    loc, mst, prow_s, prow_r, mrow_s, mrow_r, pc_s, pc_r, pcs_s, pcs_r, x_s, x_r, z_s, z_r,
    red_s, red_r, reds_s, reds_r, fx_s, fx_r, ft_s, ft_r, rx_s, rx_r, qx_s, qx_r, sum_s, sum_r,
):
    leaf = lax.axis_index("leaf")
    grid = lax.axis_index("grid")
    z, a = leaf // 2, leaf % 2
    y, b, c = grid // 4, (grid // 2) % 2, grid % 2
    front, idx = z // 2, leaf % 4
    same = a == b
    here_rows = pl.ds(pl.multiple_of(c * 256, 256), 256)
    sib_rows = pl.ds(pl.multiple_of((1 - c) * 256, 256), 256)

    def at_idx(i):
        return (front * 4 + i, grid)

    def at_y(k):
        return (leaf, flip(y, k) * 4 + grid % 4)

    def at_z(k):
        return (flip(z, k) * 2 + a, grid)

    sibling = (leaf, grid + 1 - 2 * c)
    partner = (leaf, y * 4 + (1 - b) * 2 + c)

    def remote(src, dst, ss, rs, dev):
        return pltpu.make_async_remote_copy(
            src_ref=src, dst_ref=dst, send_sem=ss, recv_sem=rs, device_id=dev, device_id_type=MESH
        )

    bar = pltpu.get_barrier_semaphore()

    def greet(dev):
        pl.semaphore_signal(bar, inc=1, device_id=dev, device_id_type=MESH)

    @pl.loop(1, 16)
    def _(k):
        greet((leaf, (grid + k) % 16))

    for k in range(1, 4):
        greet(at_z(k))
        greet(at_idx(flip(idx, k)))
        greet(((z * 2) + ((a * 2 + b + k) % 4) // 2, y * 4 + ((a * 2 + b + k) % 4) % 2 * 2 + c))
    on_turn = idx == y
    for yy in range(4):
        for cc in range(2):
            @pl.when(jnp.logical_not(on_turn & (yy == y) & (cc == c)))
            def _():
                greet((front * 4 + y, yy * 4 + b * 2 + cc))
    pl.semaphore_wait(bar, 15 + 9 + 8 - on_turn.astype(jnp.int32))

    prow = [None] + [
        remote(p_hbm, p_row.at[k], prow_s.at[k], prow_r.at[k], at_idx(flip(idx, k))) for k in range(1, 4)
    ]
    for k in (2, 3, 1):
        prow[k].start()
    step_one = remote(s_hbm, s_buf.at[0, pl.ds(pl.multiple_of(b * 256, 256), 256)], x_s.at[0], x_r.at[0],
                      device(z, a, y, a, c))
    step_two = remote(s_hbm, s_buf.at[0, pl.ds(pl.multiple_of(b * 256, 256), 256)], x_s.at[1], x_r.at[1],
                      device(z, 1 - a, y, a, c))
    step_out = remote(s_hbm, s_buf.at[0, pl.ds(pl.multiple_of(b * 256, 256), 256)], x_s.at[0], x_r.at[0],
                      device(z, 1 - a, y, a, c))
    own_s = pltpu.make_async_copy(s_hbm, s_buf.at[0, pl.ds(pl.multiple_of(b * 256, 256), 256)], loc.at[0])

    @pl.when(same)
    def _():
        own_s.start()
        step_out.start()

    @pl.when(jnp.logical_not(same))
    def _():
        step_one.start()
        step_two.start()

    pcol = [None] + [
        remote(p_hbm, p_col.at[k, here_rows], pc_s.at[k], pc_r.at[k], at_y(k)) for k in range(1, 4)
    ]
    for k in (1, 3, 2):
        pcol[k].start()
    own_prow = pltpu.make_async_copy(p_hbm, p_row.at[0], loc.at[1])
    own_pcol = pltpu.make_async_copy(p_hbm, p_col.at[0, here_rows], loc.at[2])
    own_mrow = pltpu.make_async_copy(minv_hbm, m_row.at[0], loc.at[3])
    own_l = pltpu.make_async_copy(l_hbm, l_own, loc.at[4])
    own_m = pltpu.make_async_copy(
        m_hbm.at[pl.ds(pl.multiple_of(grid * 128, 128), 128)], m_own, loc.at[5])
    own_prow.start()

    def m_load(k, slot):
        start = pl.multiple_of(flip(idx, k) * 512, 512)
        return pltpu.make_async_copy(m_hbm.at[pl.ds(start, 512)], m_stage.at[slot], mst.at[slot])

    m_load(0, 0).start()
    m_load(1, 1).start()
    own_l.start()
    own_pcol.start()
    own_mrow.start()
    own_m.start()
    pcs = [remote(p_hbm if k == 0 else p_col.at[k, here_rows], p_col.at[k, here_rows],
                  pcs_s.at[k], pcs_r.at[k], sibling) for k in range(4)]
    pcs[0].start()

    def split_m(slot):
        @pl.loop(0, 16)
        def _(i):
            rows = pl.ds(pl.multiple_of(i * 32, 32), 32)
            hi, lo = high_low(m_stage[slot, rows])
            b_hi[rows] = hi
            b_lo[rows] = lo

    def accumulate(acc, m, lhs, rhs_hi, rhs_lo, n, first):
        @pl.loop(0, n // 256)
        def _(j):
            cols = pl.ds(pl.multiple_of(j * 256, 256), 256)
            hi = rhs_hi[:, cols]
            part = jnp.dot(lhs[0:m], hi, preferred_element_type=F32)
            part += jnp.dot(lhs[m:2 * m], hi, preferred_element_type=F32)
            part += jnp.dot(lhs[0:m], rhs_lo[:, cols], preferred_element_type=F32)
            if first:
                acc[:, cols] = part
            else:
                acc[:, cols] += part

    zs = [None] + [
        remote(s_buf.at[0], s_buf.at[k], z_s.at[k], z_r.at[k], at_z(k)) for k in range(1, 4)
    ]

    mrow = [None] + [
        remote(minv_hbm, m_row.at[k], mrow_s.at[k], mrow_r.at[k], at_idx(flip(idx, k))) for k in range(1, 4)
    ]

    for k in range(4):
        if k == 0:
            own_prow.wait()
        else:
            prow[k].wait_recv()
        m_load(k, k % 2).wait()
        split_m(k % 2)
        if k + 2 < 4:
            m_load(k + 2, k % 2).start()
        hi, lo = high_low(p_row[k])
        a_tmp[0:256] = hi
        a_tmp[256:512] = lo
        accumulate(red_acc, 256, a_tmp, b_hi, b_lo, 1024, k == 0)
        if k == 0:
            @pl.when(same)
            def _():
                own_s.wait()
                step_one.wait_recv()

            @pl.when(jnp.logical_not(same))
            def _():
                step_one.wait_recv()
                step_two.wait_recv()
            for kz in (3, 2, 1):
                zs[kz].start()
    own_l.wait()
    front_q = leaf // 2
    for i in range(2):
        keep = pattern[front_q, grid * 2 + i].astype(F32)
        rows = slice(i * 128, i * 128 + 128)
        l_own[rows] = l_own[rows] * keep
    red_acc[...] = l_own[...] - red_acc[...]
    red[0, here_rows] = red_acc[...]
    ry = [None] + [
        remote(red_acc, red.at[k, here_rows], red_s.at[k], red_r.at[k], at_y(k)) for k in range(1, 4)
    ]
    rs = [remote(red_acc if k == 0 else red.at[k, here_rows], red.at[k, here_rows],
                 reds_s.at[k], reds_r.at[k], sibling) for k in range(4)]
    for k in (1, 3, 2):
        ry[k].start()
    rs[0].start()
    for k in (2, 3, 1):
        mrow[k].start()
    for k in range(1, 4):
        pcol[k].wait_recv()
        pcs[k].start()
    own_pcol.wait()
    for k in range(4):
        pcs[k].wait_recv()

    def split_s(slot):
        @pl.loop(0, 16)
        def _(i):
            rows = pl.ds(pl.multiple_of(i * 32, 32), 32)
            hi, lo = high_low(s_buf[slot, rows])
            s_split[slot, rows] = hi
            s_split[slot, pl.ds(pl.multiple_of(512 + i * 32, 32), 32)] = lo

    for n, k in enumerate((0, 3, 1, 2)):
        if k:
            zs[k].wait_recv()
        split_s(k)
        far = flip(z, k)
        for ky in range(4):
            @pl.when(flip(y, ky) == far)
            def _():
                hi, lo = high_low(p_col[ky])
                pc_hi[...] = hi
                pc_lo[...] = lo
        accumulate(f_part, 512, s_split.at[k], pc_hi, pc_lo, 512, n == 0)
    other_rows = pl.ds(pl.multiple_of((1 - b) * 256, 256), 256)
    own_rows = pl.ds(pl.multiple_of(b * 256, 256), 256)
    fx = remote(f_part.at[other_rows], f_recv, fx_s.at[0], fx_r.at[0], partner)
    fx.start()

    def root_chunk(k, first):
        if k:
            ry[k].wait_recv()
            rs[k].start()
        rs[k].wait_recv()

        @pl.loop(0, 16)
        def _(i):
            rows = pl.ds(pl.multiple_of(i * 32, 32), 32)
            hi, lo = high_low(red[k, rows])
            red_hi[k, rows] = hi
            red_lo[k, rows] = lo

        far = flip(y, k)
        for kz in range(4):
            @pl.when(flip(z, kz) == far)
            def _():
                accumulate(r_part, 512, s_split.at[kz], red_hi.at[k], red_lo.at[k], 1024, first)

    root_chunk(0, True)

    fx.wait_recv()
    f_all = f_part[own_rows] + f_recv[...]
    f_out[...] = -f_all
    turned = f_all.T
    for cc in range(2):
        for bb in range(2):
            ft_src[cc, bb * 128:bb * 128 + 128] = turned[bb * 256 + cc * 128:bb * 256 + cc * 128 + 128]
    own_ft = pltpu.make_async_copy(ft_src.at[c], ft.at[y, c], loc.at[6])

    def ft_copy(i, cc):
        return remote(ft_src.at[cc], ft.at[y, c], ft_s.at[i, cc], ft_r.at[y, c],
                      (front * 4 + i, idx * 4 + b * 2 + cc))

    for i in range(4):
        for cc in range(2):
            mine = on_turn & (i == idx) & (cc == c)

            @pl.when(mine)
            def _():
                own_ft.start()

            @pl.when(jnp.logical_not(mine))
            def _():
                ft_copy(i, cc).start()

    own_mrow.wait()
    mid = jnp.sum(p_row[0] * f_all, axis=0, keepdims=True)
    row_at = grid * 128 + lax.broadcasted_iota(jnp.int32, (128, 512), 0)
    col_at = idx * 512 + lax.broadcasted_iota(jnp.int32, (128, 512), 1)
    mid += jnp.sum(jnp.where(row_at == col_at, m_row[0], 0.0), axis=0, keepdims=True)
    for i in range(4):
        sums[0, 8 + i:9 + i] = mid[:, i * 128:i * 128 + 128]
        sums[0, 12 + i:13 + i] = jnp.zeros((1, 128), F32)

    for k in (1, 3, 2):
        root_chunk(k, False)
    rx = remote(r_part.at[other_rows], r_recv, rx_s.at[0], rx_r.at[0], partner)
    rx.start()

    m_load(0, 0).start()
    m_load(1, 1).start()
    for k in range(4):
        if k:
            mrow[k].wait_recv()
        m_load(k, k % 2).wait()
        split_m(k % 2)
        if k + 2 < 4:
            m_load(k + 2, k % 2).start()
        hi, lo = high_low(m_row[k])
        q_tmp[0:128] = hi
        q_tmp[128:256] = lo
        accumulate(mm, 128, q_tmp, b_hi, b_lo, 1024, k == 0)

    for n, k in enumerate((0, 1, 3, 2)):
        far = flip(y, k)
        for cc in range(2):
            @pl.when(on_turn & (k == 0) & (cc == c))
            def _():
                own_ft.wait()

            @pl.when(jnp.logical_not(on_turn & (k == 0) & (cc == c)))
            def _():
                remote(ft_src.at[cc], ft.at[far, cc], ft_s.at[0, cc], ft_r.at[far, cc], partner).wait_recv()
            hi, lo = high_low(ft[far, cc])
            a_tmp[0:256, cc * 256:cc * 256 + 256] = hi
            a_tmp[256:512, cc * 256:cc * 256 + 256] = lo
        accumulate(q_part, 256, a_tmp, red_hi.at[k], red_lo.at[k], 1024, n == 0)
    qx = remote(q_part.at[pl.ds(pl.multiple_of((1 - b) * 128, 128), 128)], q_recv, qx_s.at[0], qx_r.at[0], partner)
    qx.start()

    rx.wait_recv()
    root = r_part[own_rows] + r_recv[...]
    root_out[...] = -root
    low = jnp.sum(l_own[...] * root, axis=0, keepdims=True)
    own_m.wait()
    qx.wait_recv()
    par = mm[...] - (q_part[pl.ds(pl.multiple_of(b * 128, 128), 128)] + q_recv[...])
    par_out[...] = -par
    low += jnp.sum(m_own[...] * par, axis=0, keepdims=True)
    for i in range(8):
        sums[0, i:i + 1] = low[:, i * 128:i * 128 + 128]

    def sum_copy(k):
        return remote(sums.at[0], sums.at[k], sum_s.at[k], sum_r.at[k], (leaf, (grid + k) % 16))

    for k in range(1, 16):
        sum_copy(k).start()
    total = sums[0]
    for k in range(1, 16):
        sum_copy(k).wait_recv()
    for k in range(1, 16):
        total += sums[k]
    mid_out[...] = total[8:16]
    low_out[...] = total[0:8] + diag_ref[...]

    for k in range(1, 4):
        prow[k].wait_send()
        pcol[k].wait_send()
        zs[k].wait_send()
        mrow[k].wait_send()
        ry[k].wait_send()
    for k in range(4):
        pcs[k].wait_send()
        rs[k].wait_send()

    @pl.when(same)
    def _():
        step_out.wait_send()

    @pl.when(jnp.logical_not(same))
    def _():
        step_one.wait_send()
        step_two.wait_send()
    fx.wait_send()
    rx.wait_send()
    qx.wait_send()
    for i in range(4):
        for cc in range(2):
            @pl.when(jnp.logical_not(on_turn & (i == idx) & (cc == c)))
            def _():
                ft_copy(i, cc).wait_send()
    for k in range(1, 16):
        sum_copy(k).wait_send()


def local(root_inverse, middle_inverse, middle_panel, lower_root, lower_middle, block_pattern, lower_diagonal):
    dma = pltpu.SemaphoreType.DMA
    vmem = pl.BlockSpec(memory_space=pltpu.VMEM)
    hbm = pl.BlockSpec(memory_space=pl.ANY)
    scratch = [
        pltpu.VMEM(shape, F32)
        for shape in (
            (4, 512, 512), (4, 512, 512), (4, 512, 1024), (4, 256, 512), (4, 128, 512), (4, 2, 256, 256),
            (512, 512), (2, 256, 256), (256, 512), (512, 1024), (256, 1024), (256, 1024), (128, 1024),
            (2, 512, 1024), (256, 1024), (128, 1024), (128, 1024), (256, 1024), (16, 16, 128),
        )
    ] + [
        pltpu.VMEM(shape, BF16)
        for shape in (
            (4, 1024, 512), (4, 512, 1024), (4, 512, 1024), (512, 1024), (512, 1024),
            (512, 512), (512, 512), (512, 512), (256, 512),
        )
    ] + [
        dma((7,)), dma((2,)), dma((4,)), dma((4,)), dma((4,)), dma((4,)), dma((4,)), dma((4,)), dma((4,)), dma((4,)),
        dma((2,)), dma((2,)), dma((4,)), dma((4,)),
        dma((4,)), dma((4,)), dma((4,)), dma((4,)), dma((1,)), dma((1,)), dma((4, 2)), dma((4, 2)),
        dma((1,)), dma((1,)), dma((1,)), dma((1,)), dma((16,)), dma((16,)),
    ]
    first, mid, root, par, low = pl.pallas_call(
        kernel,
        out_shape=(
            jax.ShapeDtypeStruct((256, 512), F32),
            jax.ShapeDtypeStruct((8, 128), F32),
            jax.ShapeDtypeStruct((256, 1024), F32),
            jax.ShapeDtypeStruct((128, 1024), F32),
            jax.ShapeDtypeStruct((8, 128), F32),
        ),
        in_specs=[hbm, hbm, hbm, hbm, hbm, pl.BlockSpec(memory_space=pltpu.SMEM), vmem],
        out_specs=(vmem,) * 5,
        scratch_shapes=scratch,
        compiler_params=pltpu.CompilerParams(
            collective_id=0, has_side_effects=True, vmem_limit_bytes=60 * MIB
        ),
        cost_estimate=pl.CostEstimate(flops=18 * 10**9, bytes_accessed=16 * MIB, transcendentals=0),
        name="selected_inverse",
    )(
        root_inverse, middle_inverse, middle_panel, lower_root, lower_middle, block_pattern,
        lower_diagonal.reshape(8, 128),
    )
    return first, mid.reshape(1024)[:512], root, par, low.reshape(1024)


def solution(mesh):
    in_specs = (
        P("grid", "leaf"),
        P("grid", "leaf"),
        P("grid", "leaf"),
        P("grid", "leaf"),
        P(None, "leaf"),
        P(),
        P("leaf"),
    )
    out_specs = (P("grid", "leaf"), P("leaf"), P("grid", "leaf"), P("grid", "leaf"), P("leaf"))
    return jax.shard_map(local, mesh=mesh, in_specs=in_specs, out_specs=out_specs, check_vma=False)
```

```python
import functools

import jax
import jax.numpy as jnp
from jax import lax
from jax.experimental import pallas as pl
from jax.experimental.pallas import tpu as pltpu
from jax.sharding import PartitionSpec as P

MESH = pl.DeviceIdType.MESH
F32 = jnp.float32
BF16 = jnp.bfloat16
MIB = 2**20


def device(z, a, y, b, c):
    return (z * 2 + a, y * 4 + b * 2 + c)


def flip(v, k):
    if k == 0:
        return v
    if k == 1:
        return v + 1 - 2 * (v % 2)
    if k == 2:
        return (v + 2) % 4
    return 3 - v


def high_low(x):
    high = x.astype(BF16)
    low = (x - high.astype(F32)).astype(BF16)
    return high, low


def kernel(
    s_hbm, minv_hbm, p_hbm, l_hbm, m_hbm, pattern, diag_ref,
    f_out, mid_out, root_out, par_out, low_out,
    s_buf, p_col, l_buf, frow, ft, f_part, f_recv, r_part, r_recv, q_part, q_recv, t_part, t_recv, t_row,
    m_stage, m_own, tm, fm, sums,
    s_split, l_hi, l_lo, m_hi, m_lo, p_hi, p_lo, a_tmp, t_tmp, ft_split,
    loc, mst, x_s, x_r, z_s, z_r, py_s, py_r, ps_s, ps_r, ly_s, ly_r, ls_s, ls_r,
    fx_s, fx_r, fr_s, fr_r, ft_s, ft_r, rx_s, rx_r, qx_s, qx_r, tx_s, tx_r, tr_s, tr_r, sum_s, sum_r,
):
    leaf = lax.axis_index("leaf")
    grid = lax.axis_index("grid")
    z, a = leaf // 2, leaf % 2
    y, b, c = grid // 4, (grid // 2) % 2, grid % 2
    front, idx = z // 2, leaf % 4
    same = a == b
    differ = jnp.logical_not(same)
    here_rows = pl.ds(pl.multiple_of(c * 256, 256), 256)

    def half_rows(h):
        return pl.ds(pl.multiple_of(c * 256 + h * 128, 128), 128)

    def at_idx(k):
        return (front * 4 + flip(idx, k), grid)

    def at_y(k):
        return (leaf, flip(y, k) * 4 + grid % 4)

    def at_z(k):
        return (flip(z, k) * 2 + a, grid)

    sibling = (leaf, grid + 1 - 2 * c)
    partner = (leaf, y * 4 + (1 - b) * 2 + c)
    def remote(src, dst, ss, rs, dev):
        return pltpu.make_async_remote_copy(
            src_ref=src, dst_ref=dst, send_sem=ss, recv_sem=rs, device_id=dev, device_id_type=MESH
        )

    bar = pltpu.get_barrier_semaphore()

    def greet(dev):
        pl.semaphore_signal(bar, inc=1, device_id=dev, device_id_type=MESH)

    @pl.loop(1, 16)
    def _(k):
        greet((leaf, (grid + k) % 16))

    greet(at_z(1))
    greet(at_z(3))
    for k in range(1, 4):
        x = (a * 2 + b + k) % 4
        greet(device(z, x // 2, y, x % 2, c))
    pl.semaphore_wait(bar, 20)

    def own_s(h):
        return pltpu.make_async_copy(s_hbm.at[pl.ds(h * 128, 128)], s_buf.at[0, h, b], loc.at[h])

    def step(h, kind, n, dev):
        return remote(s_hbm.at[pl.ds(h * 128, 128)], s_buf.at[0, h, b], x_s.at[kind, h], x_r.at[n, h], dev)

    def step_one(h):
        return step(h, 0, 0, device(z, a, y, a, c))

    def step_two(h):
        return step(h, 1, 1, device(z, 1 - a, y, a, c))

    def step_out(h):
        return step(h, 0, 0, device(z, 1 - a, y, a, c))

    @pl.when(same)
    def _():
        for h in range(2):
            own_s(h).start()
            step_out(h).start()

    @pl.when(differ)
    def _():
        for h in range(2):
            step_one(h).start()
            step_two(h).start()

    own_l = pltpu.make_async_copy(l_hbm, l_buf.at[0, here_rows], loc.at[4])
    own_l.start()

    def y_own(src, buf, ss, rs, h, k):
        return remote(src, buf.at[k, half_rows(h)], ss.at[h, k], rs.at[h, k], at_y(k))

    def y_on(buf, ss, rs, h):
        came, way = (1, 3) if h == 0 else (3, 1)
        return remote(buf.at[came, half_rows(h)], buf.at[2, half_rows(h)], ss.at[h, 2], rs.at[h, 2], at_y(way))

    def p_own(h, k):
        return y_own(p_hbm.at[pl.ds(h * 128, 128)], p_col, py_s, py_r, h, k)

    def l_own(h, k):
        return y_own(l_buf.at[0, half_rows(h)], l_buf, ly_s, ly_r, h, k)

    for h, k in ((0, 1), (1, 3), (1, 1), (0, 3)):
        p_own(h, k).start()
    own_p = pltpu.make_async_copy(p_hbm, p_col.at[0, here_rows], loc.at[2])
    own_p.start()
    own_t = pltpu.make_async_copy(minv_hbm, t_row.at[0], loc.at[3])
    own_m = pltpu.make_async_copy(m_hbm.at[pl.ds(pl.multiple_of(grid * 128, 128), 128)], m_own, loc.at[5])
    own_t.start()
    own_m.start()

    def m_load(i):
        return pltpu.make_async_copy(m_hbm.at[pl.ds(i * 256, 256)], m_stage.at[i % 2], mst.at[i % 2])

    m_load(0).start()
    m_load(1).start()

    def p_side(k):
        return remote(p_hbm if k == 0 else p_col.at[k, here_rows], p_col.at[k, here_rows],
                      ps_s.at[k], ps_r.at[k], sibling)

    def l_side(k):
        return remote(l_buf.at[k, here_rows], l_buf.at[k, here_rows], ls_s.at[k], ls_r.at[k], sibling)

    p_side(0).start()

    own_l.wait()
    for i in range(2):
        keep = pattern[leaf // 2, grid * 2 + i].astype(F32)
        l_buf[0, half_rows(i)] = l_buf[0, half_rows(i)] * keep
    for h, k in ((0, 1), (1, 3), (1, 1), (0, 3)):
        l_own(h, k).start()
    l_side(0).start()

    def split_m(i):
        m_load(i).wait()

        @pl.loop(0, 8)
        def _(n):
            rows = pl.ds(pl.multiple_of(n * 32, 32), 32)
            to = pl.ds(pl.multiple_of(i % 2 * 256 + n * 32, 32), 32)
            hi, lo = high_low(m_stage[i % 2, rows])
            m_hi[i // 2, to] = hi
            m_lo[i // 2, to] = lo
        if i + 2 < 8:
            m_load(i + 2).start()

    def split_rows(src, hi_ref, lo_ref, k):
        for n, m in enumerate((0, 2, 1, 3)):
            @pl.loop(0, 4)
            def _(i):
                rows = pl.ds(pl.multiple_of(m * 128 + i * 32, 32), 32)
                to = pl.ds(pl.multiple_of(n * 128 + i * 32, 32), 32)
                hi, lo = high_low(src[k, rows])
                hi_ref[k, to] = hi
                lo_ref[k, to] = lo

    def split_s(k, h):
        for bb in range(2):
            hi, lo = high_low(s_buf[k, h, bb])
            for part, base in ((hi, 0), (lo, 256)):
                at = slice(base + bb * 128, base + bb * 128 + 128)
                for n, m in enumerate((0, 2, 1, 3)):
                    s_split[k, h, at, n * 128:n * 128 + 128] = part[:, m * 128:m * 128 + 128]

    def accumulate(acc, m, lhs, rhs_hi, rhs_lo, n, first, offset=0):
        @pl.loop(0, n // 256)
        def _(j):
            cols = pl.ds(pl.multiple_of(j * 256, 256), 256)
            from_cols = pl.ds(pl.multiple_of(offset + j * 256, 256), 256)
            hi = rhs_hi[:, from_cols]
            part = jnp.dot(lhs[0:m], hi, preferred_element_type=F32)
            part += jnp.dot(lhs[m:2 * m], hi, preferred_element_type=F32)
            part += jnp.dot(lhs[0:m], rhs_lo[:, from_cols], preferred_element_type=F32)
            if first:
                acc[:, cols] = part
            else:
                acc[:, cols] += part

    def z_own(h, bb, k):
        return remote(s_buf.at[0, h, bb], s_buf.at[k, h, bb], z_s.at[h, bb, k], z_r.at[h, bb, k], at_z(k))

    def z_on(h, bb):
        came, way = (1, 3) if bb == 0 else (3, 1)
        return remote(s_buf.at[came, h, bb], s_buf.at[2, h, bb], z_s.at[h, bb, 2], z_r.at[h, bb, 2], at_z(way))

    def s_here(h):
        @pl.when(same)
        def _():
            own_s(h).wait()
            step_one(h).wait_recv()

        @pl.when(differ)
        def _():
            step_one(h).wait_recv()
            step_two(h).wait_recv()
        for bb, k in ((0, 1), (1, 3), (1, 1), (0, 3)):
            z_own(h, bb, k).start()

    def s_on(h):
        z_own(h, 0, 1).wait_recv()
        z_on(h, 0).start()
        z_own(h, 1, 3).wait_recv()
        z_on(h, 1).start()

    def with_y(k, run):
        far = flip(z, k)
        for ky in range(4):
            @pl.when(flip(y, ky) == far)
            def _():
                run(ky)

    def f_chunk(h, k, first=False):
        split_s(k, h)

        def run(ky):
            accumulate(f_part.at[h], 256, s_split.at[k, h], p_hi.at[ky], p_lo.at[ky], 512, first)
        with_y(k, run)

    def f_near(h):
        for k, bb in ((1, 1), (3, 0)):
            z_own(h, bb, k).wait_recv()
            f_chunk(h, k)

    other_rows = pl.ds(pl.multiple_of((1 - b) * 128, 128), 128)
    own_rows = pl.ds(pl.multiple_of(b * 128, 128), 128)

    def fx(h):
        return remote(f_part.at[h, other_rows], f_recv.at[h], fx_s.at[h], fx_r.at[h], partner)

    def f_last(h):
        z_on(h, 0).wait_recv()
        z_on(h, 1).wait_recv()
        f_chunk(h, 2)
        fx(h).start()

    def fr(k, h):
        src = frow.at[1, h] if k == 3 else frow.at[0, h]
        return remote(src, frow.at[k, h], fr_s.at[k, h], fr_r.at[k, h], at_idx(1 if k == 1 else 2))

    def f_final(h):
        fx(h).wait_recv()
        whole = f_part[h, own_rows] + f_recv[h]
        for cc in range(2):
            for bb in range(2):
                at = bb * 256 + cc * 128
                frow[0, h, cc, :, bb * 128:bb * 128 + 128] = whole[:, at:at + 128]
        fr(1, h).start()
        fr(2, h).start()
        f_out[h * 128:h * 128 + 128] = -whole

    def ft_far(k, h, cc):
        return remote(frow.at[k, h, cc], ft.at[y, c, h], ft_s.at[h, k, cc], ft_r.at[h, y, c],
                      (leaf, flip(idx, k) * 4 + b * 2 + cc))

    def ft_near(k, h):
        return pltpu.make_async_copy(frow.at[k, h, c], ft.at[y, c, h], loc.at[6 + h])

    def ft_send(k, h):
        for cc in range(2):
            mine = (flip(idx, k) == y) & (c == cc)

            @pl.when(mine)
            def _():
                ft_near(k, h).start()

            @pl.when(jnp.logical_not(mine))
            def _():
                ft_far(k, h, cc).start()

    def fr_step(k, h):
        fr(k, h).wait_recv()
        if k == 1:
            fr(3, h).start()
        ft_send(k, h)

    def root_chunk(ky, first):
        far = flip(y, ky)
        for kz in range(4):
            @pl.when(flip(z, kz) == far)
            def _():
                for h in range(2):
                    accumulate(r_part.at[h], 256, s_split.at[kz, h], l_hi.at[ky], l_lo.at[ky], 1024, first)

    def l_ready(k):
        l_side(k).wait_recv()
        split_rows(l_buf, l_hi, l_lo, k)

    split_m(0)
    split_m(1)
    p_own(0, 1).wait_recv()
    y_on(p_col, py_s, py_r, 0).start()
    p_own(1, 3).wait_recv()
    y_on(p_col, py_s, py_r, 1).start()
    split_m(2)
    s_here(0)
    split_m(3)
    p_own(1, 1).wait_recv()
    p_side(1).start()
    p_own(0, 3).wait_recv()
    p_side(3).start()
    split_m(4)
    s_on(0)
    s_here(1)
    split_m(5)
    y_on(p_col, py_s, py_r, 0).wait_recv()
    y_on(p_col, py_s, py_r, 1).wait_recv()
    p_side(2).start()
    own_p.wait()
    split_m(6)
    split_m(7)
    for k in (0, 1, 3, 2):
        p_side(k).wait_recv()
        split_rows(p_col, p_hi, p_lo, k)
    f_chunk(0, 0, True)
    f_near(0)
    s_on(1)
    l_own(0, 1).wait_recv()
    y_on(l_buf, ly_s, ly_r, 0).start()
    l_own(1, 3).wait_recv()
    y_on(l_buf, ly_s, ly_r, 1).start()
    f_last(0)
    l_ready(0)
    f_chunk(1, 0, True)
    f_near(1)
    f_final(0)
    ft_send(0, 0)
    for k, h in ((1, 1), (3, 0)):
        l_own(h, k).wait_recv()
        l_side(k).start()
    f_last(1)
    fr_step(1, 0)
    fr_step(2, 0)
    root_chunk(0, True)
    f_final(1)
    ft_send(0, 1)
    y_on(l_buf, ly_s, ly_r, 0).wait_recv()
    y_on(l_buf, ly_s, ly_r, 1).wait_recv()
    l_side(2).start()
    l_ready(1)
    root_chunk(1, False)
    fr_step(3, 0)
    fr_step(1, 1)
    fr_step(2, 1)
    l_ready(3)
    root_chunk(3, False)
    fr_step(3, 1)
    l_ready(2)
    root_chunk(2, False)

    def rx(h):
        return remote(r_part.at[h, other_rows], r_recv.at[h], rx_s.at[h], rx_r.at[h], partner)

    for h in range(2):
        rx(h).start()

    tx = remote(t_part.at[other_rows], t_recv, tx_s.at[0], tx_r.at[0], partner)

    def tr(k):
        return remote(t_row.at[1] if k == 3 else t_row.at[0], t_row.at[k], tr_s.at[k], tr_r.at[k],
                      at_idx(1 if k == 1 else 2))

    def t_chunk(h, k, first):
        far = flip(y, k)
        for cc in range(2):
            came = remote(frow.at[0, h, cc], ft.at[far, cc, h], ft_s.at[h, 0, cc], ft_r.at[h, far, cc], sibling)
            if k == 0:
                @pl.when(c == cc)
                def _():
                    ft_near(0, h).wait()

                @pl.when(c != cc)
                def _():
                    came.wait_recv()
            else:
                came.wait_recv()
            hi, lo = high_low(ft[far, cc, h].T)
            ft_split[h, k, 0:256, cc * 128:cc * 128 + 128] = hi
            ft_split[h, k, 256:512, cc * 128:cc * 128 + 128] = lo
        rows = slice(h * 256, h * 256 + 256)
        accumulate(t_part, 256, ft_split.at[h, k], p_hi.at[k, rows], p_lo.at[k, rows], 512, first)

    def q_chunk(h, k, first):
        rows = slice(h * 256, h * 256 + 256)
        accumulate(q_part, 256, ft_split.at[h, k], l_hi.at[k, rows], l_lo.at[k, rows], 1024, first)

    for k in (0, 1, 3, 2):
        t_chunk(0, k, k == 0)

    for k in range(4):
        for h in range(2):
            for cc in range(2):
                hi, lo = high_low(frow[k, h, cc])
                for bb in range(2):
                    at = bb * 256 + cc * 128
                    part = slice(bb * 128, bb * 128 + 128)
                    a_tmp[h * 128:h * 128 + 128, at:at + 128] = hi[:, part]
                    a_tmp[256 + h * 128:256 + h * 128 + 128, at:at + 128] = lo[:, part]
        accumulate(fm, 256, a_tmp, m_hi.at[flip(idx, k)], m_lo.at[flip(idx, k)], 1024, k == 0)
    for k in (0, 1, 3, 2):
        t_chunk(1, k, False)
    tx.start()
    for h in range(2):
        for k in range(4):
            q_chunk(h, k, h + k == 0)
    own_t.wait()
    tx.wait_recv()
    t_row[0] = t_row[0] + (t_part[own_rows] + t_recv[...])
    tr(1).start()
    tr(2).start()
    qx = remote(q_part.at[other_rows], q_recv, qx_s.at[0], qx_r.at[0], partner)
    qx.start()

    row_at = grid * 128 + lax.broadcasted_iota(jnp.int32, (128, 512), 0)
    col_at = idx * 512 + lax.broadcasted_iota(jnp.int32, (128, 512), 1)
    mid = jnp.sum(jnp.where(row_at == col_at, t_row[0], 0.0), axis=0, keepdims=True)
    for i in range(4):
        sums[0, 8 + i:9 + i] = mid[:, i * 128:i * 128 + 128]
        sums[0, 12 + i:13 + i] = jnp.zeros((1, 128), F32)

    for k in range(4):
        if k:
            tr(k).wait_recv()
        if k == 1:
            tr(3).start()
        hi, lo = high_low(t_row[k])
        t_tmp[0:128] = hi
        t_tmp[128:256] = lo
        accumulate(tm, 128, t_tmp, m_hi.at[flip(idx, k)], m_lo.at[flip(idx, k)], 1024, k == 0)

    low = jnp.zeros((1, 1024), F32)
    for h in range(2):
        rx(h).wait_recv()
        rows = slice(h * 128, h * 128 + 128)
        root = r_part[h, own_rows] + r_recv[h] - fm[rows]
        root_out[rows] = -root
        low += jnp.sum(l_buf[0, half_rows(h)] * root, axis=0, keepdims=True)
    own_m.wait()
    qx.wait_recv()
    par = tm[...] - (q_part[own_rows] + q_recv[...])
    par_out[...] = -par
    low += jnp.sum(m_own[...] * par, axis=0, keepdims=True)
    for i in range(8):
        sums[0, i:i + 1] = low[:, i * 128:i * 128 + 128]

    def sum_copy(k):
        return remote(sums.at[0], sums.at[k], sum_s.at[k], sum_r.at[k], (leaf, (grid + k) % 16))

    for k in range(1, 16):
        sum_copy(k).start()
    total = sums[0]
    for k in range(1, 16):
        sum_copy(k).wait_recv()
    for k in range(1, 16):
        total += sums[k]
    mid_out[...] = total[8:16]
    low_out[...] = total[0:8] + diag_ref[...]

    @pl.when(same)
    def _():
        for h in range(2):
            step_out(h).wait_send()

    @pl.when(differ)
    def _():
        for h in range(2):
            step_one(h).wait_send()
            step_two(h).wait_send()
    for h in range(2):
        for k in (1, 3):
            p_own(h, k).wait_send()
            l_own(h, k).wait_send()
            for bb in range(2):
                z_own(h, bb, k).wait_send()
        y_on(p_col, py_s, py_r, h).wait_send()
        y_on(l_buf, ly_s, ly_r, h).wait_send()
        for bb in range(2):
            z_on(h, bb).wait_send()
    for k in range(4):
        p_side(k).wait_send()
        l_side(k).wait_send()
    for h in range(2):
        fx(h).wait_send()
        rx(h).wait_send()
        for k in range(4):
            if k:
                fr(k, h).wait_send()
            for cc in range(2):
                @pl.when(jnp.logical_not((flip(idx, k) == y) & (c == cc)))
                def _():
                    ft_far(k, h, cc).wait_send()
    tx.wait_send()
    for k in range(1, 4):
        tr(k).wait_send()
    qx.wait_send()
    for k in range(1, 16):
        sum_copy(k).wait_send()


def local(root_inverse, middle_inverse, middle_panel, lower_root, lower_middle, block_pattern, lower_diagonal):
    dma = pltpu.SemaphoreType.DMA
    vmem = pl.BlockSpec(memory_space=pltpu.VMEM)
    hbm = pl.BlockSpec(memory_space=pl.ANY)
    scratch = [
        pltpu.VMEM(shape, F32)
        for shape in (
            (4, 2, 2, 128, 512), (4, 512, 512), (4, 512, 1024), (4, 2, 2, 128, 256), (4, 2, 2, 128, 256),
            (2, 256, 512), (2, 128, 512), (2, 256, 1024), (2, 128, 1024), (256, 1024), (128, 1024),
            (256, 512), (128, 512), (4, 128, 512),
            (2, 256, 1024), (128, 1024), (128, 1024), (256, 1024), (16, 16, 128),
        )
    ] + [
        pltpu.VMEM(shape, BF16)
        for shape in (
            (4, 2, 512, 512), (4, 512, 1024), (4, 512, 1024), (4, 512, 1024), (4, 512, 1024),
            (4, 512, 512), (4, 512, 512), (512, 512), (256, 512), (2, 4, 512, 256),
        )
    ] + [
        dma(shape)
        for shape in (
            (8,), (2,), (2, 2), (2, 2), (2, 2, 4), (2, 2, 4), (2, 4), (2, 4), (4,), (4,), (2, 4), (2, 4), (4,), (4,),
            (2,), (2,), (4, 2), (4, 2), (2, 4, 2), (2, 4, 2), (2,), (2,), (1,), (1,), (1,), (1,), (4,), (4,),
            (16,), (16,),
        )
    ]
    first, mid, root, par, low = pl.pallas_call(
        kernel,
        out_shape=(
            jax.ShapeDtypeStruct((256, 512), F32),
            jax.ShapeDtypeStruct((8, 128), F32),
            jax.ShapeDtypeStruct((256, 1024), F32),
            jax.ShapeDtypeStruct((128, 1024), F32),
            jax.ShapeDtypeStruct((8, 128), F32),
        ),
        in_specs=[hbm, hbm, hbm, hbm, hbm, pl.BlockSpec(memory_space=pltpu.SMEM), vmem],
        out_specs=(vmem,) * 5,
        scratch_shapes=scratch,
        compiler_params=pltpu.CompilerParams(
            collective_id=0, has_side_effects=True, vmem_limit_bytes=62 * MIB
        ),
        cost_estimate=pl.CostEstimate(flops=20 * 10**9, bytes_accessed=16 * MIB, transcendentals=0),
        name="selected_inverse",
    )(
        root_inverse, middle_inverse, middle_panel, lower_root, lower_middle, block_pattern,
        lower_diagonal.reshape(8, 128),
    )
    return first, mid.reshape(1024)[:512], root, par, low.reshape(1024)


def solution(mesh):
    in_specs = (
        P("grid", "leaf"),
        P("grid", "leaf"),
        P("grid", "leaf"),
        P("grid", "leaf"),
        P(None, "leaf"),
        P(),
        P("leaf"),
    )
    out_specs = (P("grid", "leaf"), P("leaf"), P("grid", "leaf"), P("grid", "leaf"), P("leaf"))
    return jax.shard_map(local, mesh=mesh, in_specs=in_specs, out_specs=out_specs, check_vma=False)
```

```python
import functools

import jax
import jax.numpy as jnp
from jax import lax
from jax.experimental import pallas as pl
from jax.experimental.pallas import tpu as pltpu
from jax.sharding import PartitionSpec as P

MESH = pl.DeviceIdType.MESH
F32 = jnp.float32
BF16 = jnp.bfloat16
MIB = 2**20


def device(z, a, y, b, c):
    return (z * 2 + a, y * 4 + b * 2 + c)


def flip(v, k):
    if k == 0:
        return v
    if k == 1:
        return v + 1 - 2 * (v % 2)
    if k == 2:
        return (v + 2) % 4
    return 3 - v


def high_low(x):
    high = x.astype(BF16)
    low = (x - high.astype(F32)).astype(BF16)
    return high, low


def kernel(
    s_hbm, minv_hbm, p_hbm, l_hbm, m_hbm, pattern, diag_ref,
    f_hbm, root_hbm, par_hbm, sum_out,
    s_buf, p_col, l_buf, frow, ft, f_part, f_recv, r_part, r_recv, q_part, q_recv, t_part, t_recv, t_row,
    m_stage, m_own, tm, fm, sums, relay, f_out,
    s_split, l_hi, l_lo, m_hi, m_lo, p_hi, p_lo, a_tmp, t_tmp, ft_split,
    loc, mst, x_s, x_r, z_s, z_r, py_s, py_r, ps_s, ps_r, ly_s, ly_r, ls_s, ls_r,
    fx_s, fx_r, fr_s, fr_r, ft_s, ft_r, rx_s, rx_r, qx_s, qx_r, tx_s, tx_r, tr_s, tr_r, sum_s, sum_r,
):
    leaf = lax.axis_index("leaf")
    grid = lax.axis_index("grid")
    z, a = leaf // 2, leaf % 2
    y, b, c = grid // 4, (grid // 2) % 2, grid % 2
    front, idx = z // 2, leaf % 4
    same = a == b
    differ = jnp.logical_not(same)
    here_rows = pl.ds(pl.multiple_of(c * 256, 256), 256)

    def half_rows(h):
        return pl.ds(pl.multiple_of(c * 256 + h * 128, 128), 128)

    def at_idx(k):
        return (front * 4 + flip(idx, k), grid)

    def at_y(k):
        return (leaf, flip(y, k) * 4 + grid % 4)

    def at_z(k):
        return (flip(z, k) * 2 + a, grid)

    sibling = (leaf, grid + 1 - 2 * c)
    partner = (leaf, y * 4 + (1 - b) * 2 + c)
    def remote(src, dst, ss, rs, dev):
        return pltpu.make_async_remote_copy(
            src_ref=src, dst_ref=dst, send_sem=ss, recv_sem=rs, device_id=dev, device_id_type=MESH
        )

    bar = pltpu.get_barrier_semaphore()

    def greet(dev):
        pl.semaphore_signal(bar, inc=1, device_id=dev, device_id_type=MESH)

    @pl.loop(1, 16)
    def _(k):
        greet((leaf, (grid + k) % 16))

    greet(at_z(1))
    greet(at_z(3))
    for k in range(1, 4):
        x = (a * 2 + b + k) % 4
        greet(device(z, x // 2, y, x % 2, c))
    pl.semaphore_wait(bar, 20)

    def own_s(h):
        return pltpu.make_async_copy(s_hbm.at[pl.ds(h * 128, 128)], s_buf.at[0, h, b], loc.at[h])

    def step(h, kind, n, dev):
        return remote(s_hbm.at[pl.ds(h * 128, 128)], s_buf.at[0, h, b], x_s.at[kind, h], x_r.at[n, h], dev)

    def step_one(h):
        return step(h, 0, 0, device(z, a, y, a, c))

    def step_two(h):
        return step(h, 1, 1, device(z, 1 - a, y, a, c))

    def step_out(h):
        return remote(s_hbm.at[pl.ds(h * 128, 128)], relay.at[h], x_s.at[0, h], x_r.at[1, h],
                      device(z, 1 - a, y, 1 - b, c))

    def step_on(h):
        return remote(relay.at[h], s_buf.at[0, h, 1 - b], x_s.at[1, h], x_r.at[0, h], device(z, a, y, 1 - b, c))

    def step_start(h):
        @pl.when(same)
        def _():
            own_s(h).start()
            step_out(h).start()

        @pl.when(differ)
        def _():
            step_one(h).start()
            step_two(h).start()

    def step_relay(h):
        @pl.when(same)
        def _():
            step_out(h).wait_recv()
            step_on(h).start()

    step_start(0)

    own_l = pltpu.make_async_copy(l_hbm, l_buf.at[0, here_rows], loc.at[4])
    own_l.start()

    def y_own(src, buf, ss, rs, h, k):
        return remote(src, buf.at[k, half_rows(h)], ss.at[h, k], rs.at[h, k], at_y(k))

    def y_on(buf, ss, rs, h):
        came, way = (1, 3) if h == 0 else (3, 1)
        return remote(buf.at[came, half_rows(h)], buf.at[2, half_rows(h)], ss.at[h, 2], rs.at[h, 2], at_y(way))

    def p_own(h, k):
        return y_own(p_hbm.at[pl.ds(h * 128, 128)], p_col, py_s, py_r, h, k)

    def l_own(h, k):
        return y_own(l_buf.at[0, half_rows(h)], l_buf, ly_s, ly_r, h, k)

    for h, k in ((0, 1), (1, 3), (1, 1), (0, 3)):
        p_own(h, k).start()
    own_p = pltpu.make_async_copy(p_hbm, p_col.at[0, here_rows], loc.at[2])
    own_p.start()
    own_t = pltpu.make_async_copy(minv_hbm, t_row.at[0], loc.at[3])
    own_m = pltpu.make_async_copy(m_hbm.at[pl.ds(pl.multiple_of(grid * 128, 128), 128)], m_own, loc.at[5])
    own_t.start()
    own_m.start()

    def m_load(i):
        return pltpu.make_async_copy(m_hbm.at[pl.ds(i * 256, 256)], m_stage.at[i % 2], mst.at[i % 2])

    m_load(0).start()
    m_load(1).start()

    def p_side(k):
        return remote(p_hbm if k == 0 else p_col.at[k, here_rows], p_col.at[k, here_rows],
                      ps_s.at[k], ps_r.at[k], sibling)

    def l_side(k):
        return remote(l_buf.at[k, here_rows], l_buf.at[k, here_rows], ls_s.at[k], ls_r.at[k], sibling)

    p_side(0).start()

    own_l.wait()
    for i in range(2):
        keep = pattern[leaf // 2, grid * 2 + i].astype(F32)
        l_buf[0, half_rows(i)] = l_buf[0, half_rows(i)] * keep

    def split_m(i):
        m_load(i).wait()

        @pl.loop(0, 8)
        def _(n):
            rows = pl.ds(pl.multiple_of(n * 32, 32), 32)
            to = pl.ds(pl.multiple_of(i % 2 * 256 + n * 32, 32), 32)
            hi, lo = high_low(m_stage[i % 2, rows])
            m_hi[i // 2, to] = hi
            m_lo[i // 2, to] = lo
        if i + 2 < 8:
            m_load(i + 2).start()

    def split_rows(src, hi_ref, lo_ref, k):
        for n, m in enumerate((0, 2, 1, 3)):
            @pl.loop(0, 4)
            def _(i):
                rows = pl.ds(pl.multiple_of(m * 128 + i * 32, 32), 32)
                to = pl.ds(pl.multiple_of(n * 128 + i * 32, 32), 32)
                hi, lo = high_low(src[k, rows])
                hi_ref[k, to] = hi
                lo_ref[k, to] = lo

    def split_s(k, h):
        for bb in range(2):
            hi, lo = high_low(s_buf[k, h, bb])
            for part, base in ((hi, 0), (lo, 256)):
                at = slice(base + bb * 128, base + bb * 128 + 128)
                for n, m in enumerate((0, 2, 1, 3)):
                    s_split[k, h, at, n * 128:n * 128 + 128] = part[:, m * 128:m * 128 + 128]

    def accumulate(acc, m, lhs, rhs_hi, rhs_lo, first):
        hi = rhs_hi[...]
        part = jnp.dot(lhs[0:m], hi, preferred_element_type=F32)
        part += jnp.dot(lhs[m:2 * m], hi, preferred_element_type=F32)
        part += jnp.dot(lhs[0:m], rhs_lo[...], preferred_element_type=F32)
        if first:
            acc[...] = part
        else:
            acc[...] += part

    def z_own(h, bb, k):
        return remote(s_buf.at[0, h, bb], s_buf.at[k, h, bb], z_s.at[h, bb, k], z_r.at[h, bb, k], at_z(k))

    def z_on(h, bb):
        came, way = (1, 3) if bb == 0 else (3, 1)
        return remote(s_buf.at[came, h, bb], s_buf.at[2, h, bb], z_s.at[h, bb, 2], z_r.at[h, bb, 2], at_z(way))

    def s_here(h):
        @pl.when(same)
        def _():
            own_s(h).wait()
            step_one(h).wait_recv()

        @pl.when(differ)
        def _():
            step_one(h).wait_recv()
            step_two(h).wait_recv()
        for bb, k in ((0, 1), (1, 3), (1, 1), (0, 3)):
            z_own(h, bb, k).start()

    def s_on(h):
        z_own(h, 0, 1).wait_recv()
        z_on(h, 0).start()
        z_own(h, 1, 3).wait_recv()
        z_on(h, 1).start()

    def with_y(k, run):
        far = flip(z, k)
        for ky in range(4):
            @pl.when(flip(y, ky) == far)
            def _():
                run(ky)

    def f_chunk(h, k, first=False):
        split_s(k, h)

        def run(ky):
            accumulate(f_part.at[h], 256, s_split.at[k, h], p_hi.at[ky], p_lo.at[ky], first)
        with_y(k, run)

    def f_near(h):
        for k, bb in ((1, 1), (3, 0)):
            z_own(h, bb, k).wait_recv()
            f_chunk(h, k)

    other_rows = pl.ds(pl.multiple_of((1 - b) * 128, 128), 128)
    own_rows = pl.ds(pl.multiple_of(b * 128, 128), 128)

    def fx(h):
        return remote(f_part.at[h, other_rows], f_recv.at[h], fx_s.at[h], fx_r.at[h], partner)

    def f_last(h):
        z_on(h, 0).wait_recv()
        z_on(h, 1).wait_recv()
        f_chunk(h, 2)
        fx(h).start()

    def fr(k, h):
        src = frow.at[1, h] if k == 3 else frow.at[0, h]
        return remote(src, frow.at[k, h], fr_s.at[k, h], fr_r.at[k, h], at_idx(1 if k == 1 else 2))

    def f_final(h):
        fx(h).wait_recv()
        whole = f_part[h, own_rows] + f_recv[h]
        for cc in range(2):
            for bb in range(2):
                at = bb * 256 + cc * 128
                frow[0, h, cc, :, bb * 128:bb * 128 + 128] = whole[:, at:at + 128]
        fr(1, h).start()
        fr(2, h).start()
        f_out[h * 128:h * 128 + 128] = -whole

    def ft_far(k, h, cc):
        return remote(frow.at[k, h, cc], ft.at[y, c, h], ft_s.at[h, k, cc], ft_r.at[h, y, c],
                      (leaf, flip(idx, k) * 4 + b * 2 + cc))

    def ft_near(k, h):
        return pltpu.make_async_copy(frow.at[k, h, c], ft.at[y, c, h], loc.at[6 + h])

    def ft_send(k, h):
        for cc in range(2):
            mine = (flip(idx, k) == y) & (c == cc)

            @pl.when(mine)
            def _():
                ft_near(k, h).start()

            @pl.when(jnp.logical_not(mine))
            def _():
                ft_far(k, h, cc).start()

    def fr_step(k, h):
        fr(k, h).wait_recv()
        if k == 1:
            fr(3, h).start()
        ft_send(k, h)

    def root_chunk(ky, first):
        far = flip(y, ky)
        for kz in range(4):
            @pl.when(flip(z, kz) == far)
            def _():
                for h in range(2):
                    accumulate(r_part.at[h], 256, s_split.at[kz, h], l_hi.at[ky], l_lo.at[ky], first)

    def l_ready(k):
        l_side(k).wait_recv()
        split_rows(l_buf, l_hi, l_lo, k)

    split_m(0)
    split_m(1)
    step_relay(0)
    step_start(1)
    split_m(2)
    p_own(0, 1).wait_recv()
    y_on(p_col, py_s, py_r, 0).start()
    p_own(1, 3).wait_recv()
    y_on(p_col, py_s, py_r, 1).start()
    s_here(0)
    split_m(3)
    step_relay(1)
    p_own(1, 1).wait_recv()
    p_side(1).start()
    p_own(0, 3).wait_recv()
    p_side(3).start()
    for h, k in ((0, 1), (1, 3), (1, 1), (0, 3)):
        l_own(h, k).start()
    l_side(0).start()
    split_m(4)
    s_on(0)
    s_here(1)
    split_m(5)
    own_p.wait()
    for k in (0, 1, 3):
        p_side(k).wait_recv()
        split_rows(p_col, p_hi, p_lo, k)
    y_on(p_col, py_s, py_r, 0).wait_recv()
    y_on(p_col, py_s, py_r, 1).wait_recv()
    p_side(2).start()
    split_m(6)
    p_side(2).wait_recv()
    split_rows(p_col, p_hi, p_lo, 2)
    f_chunk(0, 0, True)
    s_on(1)
    f_near(0)
    split_m(7)
    f_last(0)
    f_chunk(1, 0, True)
    l_ready(0)
    l_own(0, 1).wait_recv()
    y_on(l_buf, ly_s, ly_r, 0).start()
    l_own(1, 3).wait_recv()
    y_on(l_buf, ly_s, ly_r, 1).start()
    f_final(0)
    ft_send(0, 0)
    f_near(1)
    f_last(1)
    fr_step(1, 0)
    for k, h in ((1, 1), (3, 0)):
        l_own(h, k).wait_recv()
        l_side(k).start()
    root_chunk(0, True)
    fr_step(2, 0)
    f_final(1)
    f_done = pltpu.make_async_copy(f_out, f_hbm, loc.at[8])
    f_done.start()
    ft_send(0, 1)
    l_ready(1)
    fr_step(3, 0)
    root_chunk(1, False)
    fr_step(1, 1)
    l_ready(3)
    root_chunk(3, False)
    fr_step(2, 1)
    y_on(l_buf, ly_s, ly_r, 0).wait_recv()
    y_on(l_buf, ly_s, ly_r, 1).wait_recv()
    l_side(2).start()
    l_ready(2)
    fr_step(3, 1)
    root_chunk(2, False)

    def rx(h):
        return remote(r_part.at[h, other_rows], r_recv.at[h], rx_s.at[h], rx_r.at[h], partner)

    for h in range(2):
        rx(h).start()

    tx = remote(t_part.at[other_rows], t_recv, tx_s.at[0], tx_r.at[0], partner)

    def tr(k):
        return remote(t_row.at[1] if k == 3 else t_row.at[0], t_row.at[k], tr_s.at[k], tr_r.at[k],
                      at_idx(1 if k == 1 else 2))

    def t_chunk(h, k, first):
        far = flip(y, k)
        for cc in range(2):
            came = remote(frow.at[0, h, cc], ft.at[far, cc, h], ft_s.at[h, 0, cc], ft_r.at[h, far, cc], sibling)
            if k == 0:
                @pl.when(c == cc)
                def _():
                    ft_near(0, h).wait()

                @pl.when(c != cc)
                def _():
                    came.wait_recv()
            else:
                came.wait_recv()
            hi, lo = high_low(ft[far, cc, h].T)
            ft_split[h, k, 0:256, cc * 128:cc * 128 + 128] = hi
            ft_split[h, k, 256:512, cc * 128:cc * 128 + 128] = lo
        rows = slice(h * 256, h * 256 + 256)
        accumulate(t_part, 256, ft_split.at[h, k], p_hi.at[k, rows], p_lo.at[k, rows], first)

    def q_chunk(h, k, first):
        rows = slice(h * 256, h * 256 + 256)
        accumulate(q_part, 256, ft_split.at[h, k], l_hi.at[k, rows], l_lo.at[k, rows], first)

    for k in (0, 1, 3, 2):
        t_chunk(0, k, k == 0)

    for k in range(4):
        for h in range(2):
            for cc in range(2):
                hi, lo = high_low(frow[k, h, cc])
                for bb in range(2):
                    at = bb * 256 + cc * 128
                    part = slice(bb * 128, bb * 128 + 128)
                    a_tmp[h * 128:h * 128 + 128, at:at + 128] = hi[:, part]
                    a_tmp[256 + h * 128:256 + h * 128 + 128, at:at + 128] = lo[:, part]
        accumulate(fm, 256, a_tmp, m_hi.at[flip(idx, k)], m_lo.at[flip(idx, k)], k == 0)
    for k in (0, 1, 3, 2):
        q_chunk(0, k, k == 0)
    for k in (0, 1, 3, 2):
        t_chunk(1, k, False)
    tx.start()
    for k in (0, 1, 3, 2):
        q_chunk(1, k, False)
    own_t.wait()
    tx.wait_recv()
    t_row[0] = t_row[0] + (t_part[own_rows] + t_recv[...])
    tr(1).start()
    tr(2).start()
    qx = remote(q_part.at[other_rows], q_recv, qx_s.at[0], qx_r.at[0], partner)
    qx.start()

    row_at = grid * 128 + lax.broadcasted_iota(jnp.int32, (128, 512), 0)
    col_at = idx * 512 + lax.broadcasted_iota(jnp.int32, (128, 512), 1)
    mid = jnp.sum(jnp.where(row_at == col_at, t_row[0], 0.0), axis=0, keepdims=True)
    for i in range(4):
        sums[0, 8 + i:9 + i] = mid[:, i * 128:i * 128 + 128]
        sums[0, 12 + i:13 + i] = jnp.zeros((1, 128), F32)

    for k in range(4):
        if k:
            tr(k).wait_recv()
        if k == 1:
            tr(3).start()
        hi, lo = high_low(t_row[k])
        t_tmp[0:128] = hi
        t_tmp[128:256] = lo
        accumulate(tm, 128, t_tmp, m_hi.at[flip(idx, k)], m_lo.at[flip(idx, k)], k == 0)

    def root_done(h):
        return pltpu.make_async_copy(r_recv.at[h], root_hbm.at[pl.ds(h * 128, 128)], loc.at[9 + h])

    low = jnp.zeros((1, 1024), F32)
    for h in range(2):
        rx(h).wait_recv()
        rows = slice(h * 128, h * 128 + 128)
        root = r_part[h, own_rows] + r_recv[h] - fm[rows]
        r_recv[h] = -root
        root_done(h).start()
        low += jnp.sum(l_buf[0, half_rows(h)] * root, axis=0, keepdims=True)
    own_m.wait()
    qx.wait_recv()
    par = tm[...] - (q_part[own_rows] + q_recv[...])
    q_recv[...] = -par
    par_done = pltpu.make_async_copy(q_recv, par_hbm, loc.at[11])
    par_done.start()
    low += jnp.sum(m_own[...] * par, axis=0, keepdims=True)
    for i in range(8):
        sums[0, i:i + 1] = low[:, i * 128:i * 128 + 128]

    def sum_copy(k):
        return remote(sums.at[0], sums.at[k], sum_s.at[k], sum_r.at[k], (leaf, (grid + k) % 16))

    for k in range(1, 16):
        sum_copy(k).start()
    total = sums[0]
    for k in range(1, 16):
        sum_copy(k).wait_recv()
    for k in range(1, 16):
        total += sums[k]
    sum_out[0:8] = total[0:8] + diag_ref[...]
    sum_out[8:16] = total[8:16]
    f_done.wait()
    for h in range(2):
        root_done(h).wait()
    par_done.wait()

    @pl.when(same)
    def _():
        for h in range(2):
            step_out(h).wait_send()
            step_on(h).wait_send()

    @pl.when(differ)
    def _():
        for h in range(2):
            step_one(h).wait_send()
            step_two(h).wait_send()
    for h in range(2):
        for k in (1, 3):
            p_own(h, k).wait_send()
            l_own(h, k).wait_send()
            for bb in range(2):
                z_own(h, bb, k).wait_send()
        y_on(p_col, py_s, py_r, h).wait_send()
        y_on(l_buf, ly_s, ly_r, h).wait_send()
        for bb in range(2):
            z_on(h, bb).wait_send()
    for k in range(4):
        p_side(k).wait_send()
        l_side(k).wait_send()
    for h in range(2):
        fx(h).wait_send()
        rx(h).wait_send()
        for k in range(4):
            if k:
                fr(k, h).wait_send()
            for cc in range(2):
                @pl.when(jnp.logical_not((flip(idx, k) == y) & (c == cc)))
                def _():
                    ft_far(k, h, cc).wait_send()
    tx.wait_send()
    for k in range(1, 4):
        tr(k).wait_send()
    qx.wait_send()
    for k in range(1, 16):
        sum_copy(k).wait_send()


def finish(first, root, par, total_hbm, first_out, mid_out, root_out, par_out, low_out, f_buf, r_buf, q_buf, total, sem):
    pairs = ((root, r_buf, root_out), (first, f_buf, first_out), (par, q_buf, par_out))
    come = [pltpu.make_async_copy(src, buf, sem.at[0, i]) for i, (src, buf, _) in enumerate(pairs)]
    go = [pltpu.make_async_copy(buf, dst, sem.at[1, i]) for i, (_, buf, dst) in enumerate(pairs)]
    sums = pltpu.make_async_copy(total_hbm, total, sem.at[0, 3])
    for copy in come:
        copy.start()
    sums.start()
    for i in range(3):
        come[i].wait()
        go[i].start()
    sums.wait()
    for i in range(8):
        low_out[i * 128:i * 128 + 128] = total[i]
    for i in range(4):
        mid_out[i * 128:i * 128 + 128] = total[8 + i]
    for copy in go:
        copy.wait()


def local(root_inverse, middle_inverse, middle_panel, lower_root, lower_middle, block_pattern, lower_diagonal):
    dma = pltpu.SemaphoreType.DMA
    vmem = pl.BlockSpec(memory_space=pltpu.VMEM)
    hbm = pl.BlockSpec(memory_space=pl.ANY)
    scratch = [
        pltpu.VMEM(shape, F32)
        for shape in (
            (4, 2, 2, 128, 512), (4, 512, 512), (4, 512, 1024), (4, 2, 2, 128, 256), (4, 2, 2, 128, 256),
            (2, 256, 512), (2, 128, 512), (2, 256, 1024), (2, 128, 1024), (256, 1024), (128, 1024),
            (256, 512), (128, 512), (4, 128, 512),
            (2, 256, 1024), (128, 1024), (128, 1024), (256, 1024), (16, 16, 128), (2, 128, 512),
            (256, 512),
        )
    ] + [
        pltpu.VMEM(shape, BF16)
        for shape in (
            (4, 2, 512, 512), (4, 512, 1024), (4, 512, 1024), (4, 512, 1024), (4, 512, 1024),
            (4, 512, 512), (4, 512, 512), (512, 512), (256, 512), (2, 4, 512, 256),
        )
    ] + [
        dma(shape)
        for shape in (
            (12,), (2,), (2, 2), (2, 2), (2, 2, 4), (2, 2, 4), (2, 4), (2, 4), (4,), (4,), (2, 4), (2, 4), (4,), (4,),
            (2,), (2,), (4, 2), (4, 2), (2, 4, 2), (2, 4, 2), (2,), (2,), (1,), (1,), (1,), (1,), (4,), (4,),
            (16,), (16,),
        )
    ]
    blocks = tuple(jax.ShapeDtypeStruct(shape, F32) for shape in ((256, 512), (256, 1024), (128, 1024)))
    first, root, par, total = pl.pallas_call(
        kernel,
        out_shape=blocks + (jax.ShapeDtypeStruct((16, 128), F32),),
        in_specs=[hbm, hbm, hbm, hbm, hbm, pl.BlockSpec(memory_space=pltpu.SMEM), vmem],
        out_specs=(hbm, hbm, hbm, vmem),
        scratch_shapes=scratch,
        compiler_params=pltpu.CompilerParams(
            collective_id=0, has_side_effects=True, vmem_limit_bytes=62 * MIB
        ),
        cost_estimate=pl.CostEstimate(flops=20 * 10**9, bytes_accessed=16 * MIB, transcendentals=0),
        name="selected_inverse",
    )(
        root_inverse, middle_inverse, middle_panel, lower_root, lower_middle, block_pattern,
        lower_diagonal.reshape(8, 128),
    )
    return pl.pallas_call(
        finish,
        out_shape=(
            blocks[0], jax.ShapeDtypeStruct((512,), F32), blocks[1], blocks[2], jax.ShapeDtypeStruct((1024,), F32),
        ),
        in_specs=[hbm, hbm, hbm, hbm],
        out_specs=(hbm, vmem, hbm, hbm, vmem),
        scratch_shapes=[pltpu.VMEM(x.shape, F32) for x in (first, root, par, total)] + [dma((2, 4))],
        compiler_params=pltpu.CompilerParams(vmem_limit_bytes=62 * MIB),
        name="hand_over",
    )(first, root, par, total)


def solution(mesh):
    in_specs = (
        P("grid", "leaf"),
        P("grid", "leaf"),
        P("grid", "leaf"),
        P("grid", "leaf"),
        P(None, "leaf"),
        P(),
        P("leaf"),
    )
    out_specs = (P("grid", "leaf"), P("leaf"), P("grid", "leaf"), P("grid", "leaf"), P("leaf"))
    return jax.shard_map(local, mesh=mesh, in_specs=in_specs, out_specs=out_specs, check_vma=False)
```

```python
import functools

import jax
import jax.numpy as jnp
from jax import lax
from jax.experimental import pallas as pl
from jax.experimental.pallas import tpu as pltpu
from jax.sharding import PartitionSpec as P

MESH = pl.DeviceIdType.MESH
F32 = jnp.float32
BF16 = jnp.bfloat16
MIB = 2**20


def device(z, a, y, b, c):
    return (z * 2 + a, y * 4 + b * 2 + c)


def flip(v, k):
    if k == 0:
        return v
    if k == 1:
        return v + 1 - 2 * (v % 2)
    if k == 2:
        return (v + 2) % 4
    return 3 - v


def either(u, v):
    return (u // 2 + v // 2) % 2 * 2 + (u + v) % 2


def high_low(x):
    high = x.astype(BF16)
    low = (x - high.astype(F32)).astype(BF16)
    return high, low


def kernel(
    s_hbm, minv_hbm, p_hbm, l_hbm, m_hbm, pattern, diag_ref,
    f_hbm, root_hbm, par_hbm, sum_out,
    s_buf, p_col, l_buf, frow, ft, f_part, f_recv, r_part, r_recv, q_part, q_recv, t_part, t_recv, t_row,
    m_stage, m_own, tm, fm, sums, relay, f_out,
    s_split, l_hi, l_lo, m_hi, m_lo, p_hi, p_lo, a_tmp, t_tmp, ft_split,
    loc, mst, x_s, x_r, z_s, z_r, py_s, py_r, ps_s, ps_r, ly_s, ly_r, ls_s, ls_r,
    fx_s, fx_r, fr_s, fr_r, ft_s, ft_r, rx_s, rx_r, qx_s, qx_r, tx_s, tx_r, tr_s, tr_r, sum_s, sum_r,
):
    leaf = lax.axis_index("leaf")
    grid = lax.axis_index("grid")
    z, a = leaf // 2, leaf % 2
    y, b, c = grid // 4, (grid // 2) % 2, grid % 2
    front, idx = z // 2, leaf % 4
    same = a == b
    differ = jnp.logical_not(same)
    here_rows = pl.ds(pl.multiple_of(c * 256, 256), 256)

    def half_rows(h):
        return pl.ds(pl.multiple_of(c * 256 + h * 128, 128), 128)

    def at_idx(k):
        return (front * 4 + flip(idx, k), grid)

    def at_y(k):
        return (leaf, flip(y, k) * 4 + grid % 4)

    def at_z(k):
        return (flip(z, k) * 2 + a, grid)

    sibling = (leaf, grid + 1 - 2 * c)
    partner = (leaf, y * 4 + (1 - b) * 2 + c)
    def remote(src, dst, ss, rs, dev):
        return pltpu.make_async_remote_copy(
            src_ref=src, dst_ref=dst, send_sem=ss, recv_sem=rs, device_id=dev, device_id_type=MESH
        )

    bar = pltpu.get_barrier_semaphore()

    def greet(dev):
        pl.semaphore_signal(bar, inc=1, device_id=dev, device_id_type=MESH)

    @pl.loop(1, 16)
    def _(k):
        greet((leaf, (grid + k) % 16))

    greet(at_z(1))
    greet(at_z(3))
    for k in range(1, 4):
        x = (a * 2 + b + k) % 4
        greet(device(z, x // 2, y, x % 2, c))
    pl.semaphore_wait(bar, 20)

    def own_s(h):
        return pltpu.make_async_copy(s_hbm.at[pl.ds(h * 128, 128)], s_buf.at[0, h, b], loc.at[h])

    def step(h, kind, n, dev):
        return remote(s_hbm.at[pl.ds(h * 128, 128)], s_buf.at[0, h, b], x_s.at[kind, h], x_r.at[n, h], dev)

    def step_one(h):
        return step(h, 0, 0, device(z, a, y, a, c))

    def step_two(h):
        return step(h, 1, 1, device(z, 1 - a, y, a, c))

    def step_out(h):
        return remote(s_hbm.at[pl.ds(h * 128, 128)], relay.at[h], x_s.at[0, h], x_r.at[1, h],
                      device(z, 1 - a, y, 1 - b, c))

    def step_on(h):
        return remote(relay.at[h], s_buf.at[0, h, 1 - b], x_s.at[1, h], x_r.at[0, h], device(z, a, y, 1 - b, c))

    def step_start(h):
        @pl.when(same)
        def _():
            own_s(h).start()
            step_out(h).start()

        @pl.when(differ)
        def _():
            step_one(h).start()
            step_two(h).start()

    def step_relay(h):
        @pl.when(same)
        def _():
            step_out(h).wait_recv()
            step_on(h).start()

    step_start(0)

    own_l = pltpu.make_async_copy(l_hbm, l_buf.at[0, here_rows], loc.at[4])
    own_l.start()

    def y_own(src, buf, ss, rs, h, k):
        return remote(src, buf.at[k, half_rows(h)], ss.at[h, k], rs.at[h, k], at_y(k))

    def y_on(buf, ss, rs, h):
        came, way = (1, 3) if h == 0 else (3, 1)
        return remote(buf.at[came, half_rows(h)], buf.at[2, half_rows(h)], ss.at[h, 2], rs.at[h, 2], at_y(way))

    def p_own(h, k):
        return y_own(p_hbm.at[pl.ds(h * 128, 128)], p_col, py_s, py_r, h, k)

    def l_own(h, k):
        return y_own(l_buf.at[0, half_rows(h)], l_buf, ly_s, ly_r, h, k)

    for h, k in ((0, 1), (1, 3), (1, 1), (0, 3)):
        p_own(h, k).start()
    own_p = pltpu.make_async_copy(p_hbm, p_col.at[0, here_rows], loc.at[2])
    own_p.start()
    own_t = pltpu.make_async_copy(minv_hbm, t_row.at[0], loc.at[3])
    own_m = pltpu.make_async_copy(m_hbm.at[pl.ds(pl.multiple_of(grid * 128, 128), 128)], m_own, loc.at[5])
    own_t.start()
    own_m.start()

    def m_load(i):
        return pltpu.make_async_copy(m_hbm.at[pl.ds(i * 256, 256)], m_stage.at[i % 2], mst.at[i % 2])

    m_load(0).start()
    m_load(1).start()

    def p_side(k):
        return remote(p_hbm if k == 0 else p_col.at[k, here_rows], p_col.at[k, here_rows],
                      ps_s.at[k], ps_r.at[k], sibling)

    def l_side(k):
        return remote(l_buf.at[k, here_rows], l_buf.at[k, here_rows], ls_s.at[k], ls_r.at[k], sibling)

    p_side(0).start()

    own_l.wait()
    for i in range(2):
        keep = pattern[leaf // 2, grid * 2 + i].astype(F32)
        l_buf[0, half_rows(i)] = l_buf[0, half_rows(i)] * keep

    def split_m(i):
        m_load(i).wait()

        @pl.loop(0, 8)
        def _(n):
            rows = pl.ds(pl.multiple_of(n * 32, 32), 32)
            to = pl.ds(pl.multiple_of(i % 2 * 256 + n * 32, 32), 32)
            hi, lo = high_low(m_stage[i % 2, rows])
            m_hi[i // 2, to] = hi
            m_lo[i // 2, to] = lo
        if i + 2 < 8:
            m_load(i + 2).start()

    def split_rows(src, hi_ref, lo_ref, k):
        for n, m in enumerate((0, 2, 1, 3)):
            @pl.loop(0, 4)
            def _(i):
                rows = pl.ds(pl.multiple_of(m * 128 + i * 32, 32), 32)
                to = pl.ds(pl.multiple_of(n * 128 + i * 32, 32), 32)
                hi, lo = high_low(src[k, rows])
                hi_ref[k, to] = hi
                lo_ref[k, to] = lo

    def split_s(k, h):
        for bb in range(2):
            hi, lo = high_low(s_buf[k, h, bb])
            for part, base in ((hi, 0), (lo, 256)):
                at = slice(base + bb * 128, base + bb * 128 + 128)
                for n, m in enumerate((0, 2, 1, 3)):
                    s_split[k, h, at, n * 128:n * 128 + 128] = part[:, m * 128:m * 128 + 128]

    def accumulate(acc, lhs, rhs_hi, rhs_lo, first):
        m, n = acc.shape
        width = min(n, 512)

        @pl.loop(0, n // width)
        def _(j):
            cols = pl.ds(pl.multiple_of(j * width, width), width)
            hi = rhs_hi[:, cols]
            part = jnp.dot(lhs[0:m], hi, preferred_element_type=F32)
            part += jnp.dot(lhs[m:2 * m], hi, preferred_element_type=F32)
            part += jnp.dot(lhs[0:m], rhs_lo[:, cols], preferred_element_type=F32)
            if first:
                acc[:, cols] = part
            else:
                acc[:, cols] += part

    def z_own(h, bb, k):
        return remote(s_buf.at[0, h, bb], s_buf.at[k, h, bb], z_s.at[h, bb, k], z_r.at[h, bb, k], at_z(k))

    def z_on(h, bb):
        came, way = (1, 3) if bb == 0 else (3, 1)
        return remote(s_buf.at[came, h, bb], s_buf.at[2, h, bb], z_s.at[h, bb, 2], z_r.at[h, bb, 2], at_z(way))

    def s_here(h):
        @pl.when(same)
        def _():
            own_s(h).wait()
            step_one(h).wait_recv()

        @pl.when(differ)
        def _():
            step_one(h).wait_recv()
            step_two(h).wait_recv()
        for bb, k in ((0, 1), (1, 3), (1, 1), (0, 3)):
            z_own(h, bb, k).start()

    def s_on(h):
        z_own(h, 0, 1).wait_recv()
        z_on(h, 0).start()
        z_own(h, 1, 3).wait_recv()
        z_on(h, 1).start()

    def f_chunk(h, k, first=False):
        split_s(k, h)
        ky = either(y, flip(z, k))
        accumulate(f_part.at[h], s_split.at[k, h], p_hi.at[ky], p_lo.at[ky], first)

    def f_near(h):
        for k, bb in ((1, 1), (3, 0)):
            z_own(h, bb, k).wait_recv()
            f_chunk(h, k)

    other_rows = pl.ds(pl.multiple_of((1 - b) * 128, 128), 128)
    own_rows = pl.ds(pl.multiple_of(b * 128, 128), 128)

    def fx(h):
        return remote(f_part.at[h, other_rows], f_recv.at[h], fx_s.at[h], fx_r.at[h], partner)

    def f_last(h):
        z_on(h, 0).wait_recv()
        z_on(h, 1).wait_recv()
        f_chunk(h, 2)
        fx(h).start()

    def fr(k, h):
        src = frow.at[1, h] if k == 3 else frow.at[0, h]
        return remote(src, frow.at[k, h], fr_s.at[k, h], fr_r.at[k, h], at_idx(1 if k == 1 else 2))

    def f_final(h):
        fx(h).wait_recv()
        whole = f_part[h, own_rows] + f_recv[h]
        for cc in range(2):
            for bb in range(2):
                at = bb * 256 + cc * 128
                frow[0, h, cc, :, bb * 128:bb * 128 + 128] = whole[:, at:at + 128]
        fr(1, h).start()
        fr(2, h).start()
        f_out[h * 128:h * 128 + 128] = -whole

    def ft_far(k, h, cc):
        return remote(frow.at[k, h, cc], ft.at[y, c, h], ft_s.at[h, k, cc], ft_r.at[h, y, c],
                      (leaf, flip(idx, k) * 4 + b * 2 + cc))

    def ft_near(k, h):
        return pltpu.make_async_copy(frow.at[k, h, c], ft.at[y, c, h], loc.at[6 + h])

    def ft_send(k, h):
        for cc in range(2):
            mine = (flip(idx, k) == y) & (c == cc)

            @pl.when(mine)
            def _():
                ft_near(k, h).start()

            @pl.when(jnp.logical_not(mine))
            def _():
                ft_far(k, h, cc).start()

    def fr_step(k, h):
        fr(k, h).wait_recv()
        if k == 1:
            fr(3, h).start()
        ft_send(k, h)

    def root_chunk(h, ky, first=False):
        kz = either(z, flip(y, ky))
        accumulate(r_part.at[h], s_split.at[kz, h], l_hi.at[ky], l_lo.at[ky], first)

    def rx(h):
        return remote(r_part.at[h, other_rows], r_recv.at[h], rx_s.at[h], rx_r.at[h], partner)

    def l_ready(k):
        l_side(k).wait_recv()
        split_rows(l_buf, l_hi, l_lo, k)

    split_m(0)
    split_m(1)
    step_relay(0)
    step_start(1)
    split_m(2)
    p_own(0, 1).wait_recv()
    y_on(p_col, py_s, py_r, 0).start()
    p_own(1, 3).wait_recv()
    y_on(p_col, py_s, py_r, 1).start()
    s_here(0)
    split_m(3)
    step_relay(1)
    p_own(1, 1).wait_recv()
    p_side(1).start()
    p_own(0, 3).wait_recv()
    p_side(3).start()
    for h, k in ((0, 1), (1, 3), (1, 1), (0, 3)):
        l_own(h, k).start()
    l_side(0).start()
    split_m(4)
    s_on(0)
    s_here(1)
    split_m(5)
    own_p.wait()
    for k in (0, 1, 3):
        p_side(k).wait_recv()
        split_rows(p_col, p_hi, p_lo, k)
    y_on(p_col, py_s, py_r, 0).wait_recv()
    y_on(p_col, py_s, py_r, 1).wait_recv()
    p_side(2).start()
    split_m(6)
    p_side(2).wait_recv()
    split_rows(p_col, p_hi, p_lo, 2)
    f_chunk(0, 0, True)
    s_on(1)
    f_near(0)
    split_m(7)
    f_last(0)
    f_chunk(1, 0, True)
    l_ready(0)
    l_own(0, 1).wait_recv()
    y_on(l_buf, ly_s, ly_r, 0).start()
    l_own(1, 3).wait_recv()
    y_on(l_buf, ly_s, ly_r, 1).start()
    f_final(0)
    ft_send(0, 0)
    root_chunk(0, 0, True)
    for k, h in ((1, 1), (3, 0)):
        l_own(h, k).wait_recv()
        l_side(k).start()
    f_near(1)
    l_ready(1)
    root_chunk(0, 1)
    l_ready(3)
    f_last(1)
    fr_step(1, 0)
    fr_step(2, 0)
    root_chunk(0, 3)
    y_on(l_buf, ly_s, ly_r, 0).wait_recv()
    y_on(l_buf, ly_s, ly_r, 1).wait_recv()
    l_side(2).start()
    f_final(1)
    f_done = pltpu.make_async_copy(f_out, f_hbm, loc.at[8])
    f_done.start()
    ft_send(0, 1)
    l_ready(2)
    root_chunk(0, 2)
    rx(0).start()
    fr_step(3, 0)
    root_chunk(1, 0, True)
    fr_step(1, 1)
    fr_step(2, 1)
    for k in (1, 3):
        root_chunk(1, k)
    fr_step(3, 1)
    root_chunk(1, 2)
    rx(1).start()

    tx = remote(t_part.at[other_rows], t_recv, tx_s.at[0], tx_r.at[0], partner)

    def tr(k):
        return remote(t_row.at[1] if k == 3 else t_row.at[0], t_row.at[k], tr_s.at[k], tr_r.at[k],
                      at_idx(1 if k == 1 else 2))

    def t_chunk(h, k, first):
        far = flip(y, k)
        for cc in range(2):
            came = remote(frow.at[0, h, cc], ft.at[far, cc, h], ft_s.at[h, 0, cc], ft_r.at[h, far, cc], sibling)
            if k == 0:
                @pl.when(c == cc)
                def _():
                    ft_near(0, h).wait()

                @pl.when(c != cc)
                def _():
                    came.wait_recv()
            else:
                came.wait_recv()
            hi, lo = high_low(ft[far, cc, h].T)
            ft_split[h, k, 0:256, cc * 128:cc * 128 + 128] = hi
            ft_split[h, k, 256:512, cc * 128:cc * 128 + 128] = lo
        rows = slice(h * 256, h * 256 + 256)
        accumulate(t_part, ft_split.at[h, k], p_hi.at[k, rows], p_lo.at[k, rows], first)

    def q_chunk(h, k, first):
        rows = slice(h * 256, h * 256 + 256)
        accumulate(q_part, ft_split.at[h, k], l_hi.at[k, rows], l_lo.at[k, rows], first)

    for k in (0, 1, 3, 2):
        t_chunk(0, k, k == 0)

    for k in range(4):
        for h in range(2):
            for cc in range(2):
                hi, lo = high_low(frow[k, h, cc])
                for bb in range(2):
                    at = bb * 256 + cc * 128
                    part = slice(bb * 128, bb * 128 + 128)
                    a_tmp[h * 128:h * 128 + 128, at:at + 128] = hi[:, part]
                    a_tmp[256 + h * 128:256 + h * 128 + 128, at:at + 128] = lo[:, part]
        accumulate(fm, a_tmp, m_hi.at[flip(idx, k)], m_lo.at[flip(idx, k)], k == 0)
    for k in (0, 1, 3, 2):
        q_chunk(0, k, k == 0)
    for k in (0, 1, 3, 2):
        t_chunk(1, k, False)
    tx.start()
    for k in (0, 1, 3, 2):
        q_chunk(1, k, False)
    own_t.wait()
    tx.wait_recv()
    t_row[0] = t_row[0] + (t_part[own_rows] + t_recv[...])
    tr(1).start()
    tr(2).start()
    qx = remote(q_part.at[other_rows], q_recv, qx_s.at[0], qx_r.at[0], partner)
    qx.start()

    row_at = grid * 128 + lax.broadcasted_iota(jnp.int32, (128, 512), 0)
    col_at = idx * 512 + lax.broadcasted_iota(jnp.int32, (128, 512), 1)
    mid = jnp.sum(jnp.where(row_at == col_at, t_row[0], 0.0), axis=0, keepdims=True)
    for i in range(4):
        sums[0, 8 + i:9 + i] = mid[:, i * 128:i * 128 + 128]
        sums[0, 12 + i:13 + i] = jnp.zeros((1, 128), F32)

    for k in range(4):
        if k:
            tr(k).wait_recv()
        if k == 1:
            tr(3).start()
        hi, lo = high_low(t_row[k])
        t_tmp[0:128] = hi
        t_tmp[128:256] = lo
        accumulate(tm, t_tmp, m_hi.at[flip(idx, k)], m_lo.at[flip(idx, k)], k == 0)

    def root_done(h):
        return pltpu.make_async_copy(r_recv.at[h], root_hbm.at[pl.ds(h * 128, 128)], loc.at[9 + h])

    low = jnp.zeros((1, 1024), F32)
    for h in range(2):
        rx(h).wait_recv()
        rows = slice(h * 128, h * 128 + 128)
        root = r_part[h, own_rows] + r_recv[h] - fm[rows]
        r_recv[h] = -root
        root_done(h).start()
        low += jnp.sum(l_buf[0, half_rows(h)] * root, axis=0, keepdims=True)
    own_m.wait()
    qx.wait_recv()
    par = tm[...] - (q_part[own_rows] + q_recv[...])
    q_recv[...] = -par
    par_done = pltpu.make_async_copy(q_recv, par_hbm, loc.at[11])
    par_done.start()
    low += jnp.sum(m_own[...] * par, axis=0, keepdims=True)
    for i in range(8):
        sums[0, i:i + 1] = low[:, i * 128:i * 128 + 128]

    def sum_copy(k):
        return remote(sums.at[0], sums.at[k], sum_s.at[k], sum_r.at[k], (leaf, (grid + k) % 16))

    for k in range(1, 16):
        sum_copy(k).start()
    total = sums[0]
    for k in range(1, 16):
        sum_copy(k).wait_recv()
    for k in range(1, 16):
        total += sums[k]
    sum_out[0:8] = total[0:8] + diag_ref[...]
    sum_out[8:16] = total[8:16]
    f_done.wait()
    for h in range(2):
        root_done(h).wait()
    par_done.wait()

    @pl.when(same)
    def _():
        for h in range(2):
            step_out(h).wait_send()
            step_on(h).wait_send()

    @pl.when(differ)
    def _():
        for h in range(2):
            step_one(h).wait_send()
            step_two(h).wait_send()
    for h in range(2):
        for k in (1, 3):
            p_own(h, k).wait_send()
            l_own(h, k).wait_send()
            for bb in range(2):
                z_own(h, bb, k).wait_send()
        y_on(p_col, py_s, py_r, h).wait_send()
        y_on(l_buf, ly_s, ly_r, h).wait_send()
        for bb in range(2):
            z_on(h, bb).wait_send()
    for k in range(4):
        p_side(k).wait_send()
        l_side(k).wait_send()
    for h in range(2):
        fx(h).wait_send()
        rx(h).wait_send()
        for k in range(4):
            if k:
                fr(k, h).wait_send()
            for cc in range(2):
                @pl.when(jnp.logical_not((flip(idx, k) == y) & (c == cc)))
                def _():
                    ft_far(k, h, cc).wait_send()
    tx.wait_send()
    for k in range(1, 4):
        tr(k).wait_send()
    qx.wait_send()
    for k in range(1, 16):
        sum_copy(k).wait_send()


def finish(first, root, par, total_hbm, first_out, mid_out, root_out, par_out, low_out, f_buf, r_buf, q_buf, total, sem):
    pairs = ((root, r_buf, root_out), (first, f_buf, first_out), (par, q_buf, par_out))
    come = [pltpu.make_async_copy(src, buf, sem.at[0, i]) for i, (src, buf, _) in enumerate(pairs)]
    go = [pltpu.make_async_copy(buf, dst, sem.at[1, i]) for i, (_, buf, dst) in enumerate(pairs)]
    sums = pltpu.make_async_copy(total_hbm, total, sem.at[0, 3])
    for copy in come:
        copy.start()
    sums.start()
    for i in range(3):
        come[i].wait()
        go[i].start()
    sums.wait()
    for i in range(8):
        low_out[i * 128:i * 128 + 128] = total[i]
    for i in range(4):
        mid_out[i * 128:i * 128 + 128] = total[8 + i]
    for copy in go:
        copy.wait()


def local(root_inverse, middle_inverse, middle_panel, lower_root, lower_middle, block_pattern, lower_diagonal):
    dma = pltpu.SemaphoreType.DMA
    vmem = pl.BlockSpec(memory_space=pltpu.VMEM)
    hbm = pl.BlockSpec(memory_space=pl.ANY)
    scratch = [
        pltpu.VMEM(shape, F32)
        for shape in (
            (4, 2, 2, 128, 512), (4, 512, 512), (4, 512, 1024), (4, 2, 2, 128, 256), (4, 2, 2, 128, 256),
            (2, 256, 512), (2, 128, 512), (2, 256, 1024), (2, 128, 1024), (256, 1024), (128, 1024),
            (256, 512), (128, 512), (4, 128, 512),
            (2, 256, 1024), (128, 1024), (128, 1024), (256, 1024), (16, 16, 128), (2, 128, 512),
            (256, 512),
        )
    ] + [
        pltpu.VMEM(shape, BF16)
        for shape in (
            (4, 2, 512, 512), (4, 512, 1024), (4, 512, 1024), (4, 512, 1024), (4, 512, 1024),
            (4, 512, 512), (4, 512, 512), (512, 512), (256, 512), (2, 4, 512, 256),
        )
    ] + [
        dma(shape)
        for shape in (
            (12,), (2,), (2, 2), (2, 2), (2, 2, 4), (2, 2, 4), (2, 4), (2, 4), (4,), (4,), (2, 4), (2, 4), (4,), (4,),
            (2,), (2,), (4, 2), (4, 2), (2, 4, 2), (2, 4, 2), (2,), (2,), (1,), (1,), (1,), (1,), (4,), (4,),
            (16,), (16,),
        )
    ]
    blocks = tuple(jax.ShapeDtypeStruct(shape, F32) for shape in ((256, 512), (256, 1024), (128, 1024)))
    first, root, par, total = pl.pallas_call(
        kernel,
        out_shape=blocks + (jax.ShapeDtypeStruct((16, 128), F32),),
        in_specs=[hbm, hbm, hbm, hbm, hbm, pl.BlockSpec(memory_space=pltpu.SMEM), vmem],
        out_specs=(hbm, hbm, hbm, vmem),
        scratch_shapes=scratch,
        compiler_params=pltpu.CompilerParams(
            collective_id=0, has_side_effects=True, vmem_limit_bytes=62 * MIB
        ),
        cost_estimate=pl.CostEstimate(flops=20 * 10**9, bytes_accessed=16 * MIB, transcendentals=0),
        name="selected_inverse",
    )(
        root_inverse, middle_inverse, middle_panel, lower_root, lower_middle, block_pattern,
        lower_diagonal.reshape(8, 128),
    )
    return pl.pallas_call(
        finish,
        out_shape=(
            blocks[0], jax.ShapeDtypeStruct((512,), F32), blocks[1], blocks[2], jax.ShapeDtypeStruct((1024,), F32),
        ),
        in_specs=[hbm, hbm, hbm, hbm],
        out_specs=(hbm, vmem, hbm, hbm, vmem),
        scratch_shapes=[pltpu.VMEM(x.shape, F32) for x in (first, root, par, total)] + [dma((2, 4))],
        compiler_params=pltpu.CompilerParams(vmem_limit_bytes=62 * MIB),
        name="hand_over",
    )(first, root, par, total)


def solution(mesh):
    in_specs = (
        P("grid", "leaf"),
        P("grid", "leaf"),
        P("grid", "leaf"),
        P("grid", "leaf"),
        P(None, "leaf"),
        P(),
        P("leaf"),
    )
    out_specs = (P("grid", "leaf"), P("leaf"), P("grid", "leaf"), P("grid", "leaf"), P("leaf"))
    return jax.shard_map(local, mesh=mesh, in_specs=in_specs, out_specs=out_specs, check_vma=False)
```

```python
import functools

import jax
import jax.numpy as jnp
from jax import lax
from jax.experimental import pallas as pl
from jax.experimental.pallas import tpu as pltpu
from jax.sharding import PartitionSpec as P

MESH = pl.DeviceIdType.MESH
F32 = jnp.float32
BF16 = jnp.bfloat16
MIB = 2**20


def device(z, a, y, b, c):
    return (z * 2 + a, y * 4 + b * 2 + c)


def flip(v, k):
    if k == 0:
        return v
    if k == 1:
        return v + 1 - 2 * (v % 2)
    if k == 2:
        return (v + 2) % 4
    return 3 - v


def either(u, v):
    return (u // 2 + v // 2) % 2 * 2 + (u + v) % 2


def high_low(x):
    high = x.astype(BF16)
    low = (x - high.astype(F32)).astype(BF16)
    return high, low


def kernel(
    s_hbm, minv_hbm, p_hbm, l_hbm, m_hbm, pattern, diag_ref,
    f_hbm, root_hbm, par_hbm, sum_out,
    s_buf, p_col, l_buf, frow, ft, f_part, f_recv, r_part, r_recv, q_part, q_recv, t_part, t_recv, t_row,
    m_stage, m_own, tm, fm, sums, relay, f_out,
    s_split, l_hi, l_lo, m_hi, m_lo, p_hi, p_lo, a_tmp, t_tmp, ft_split,
    loc, mst, x_s, x_r, z_s, z_r, py_s, py_r, ps_s, ps_r, ly_s, ly_r, ls_s, ls_r,
    fx_s, fx_r, fr_s, fr_r, ft_s, ft_r, rx_s, rx_r, qx_s, qx_r, tx_s, tx_r, tr_s, tr_r, sum_s, sum_r,
):
    leaf = lax.axis_index("leaf")
    grid = lax.axis_index("grid")
    z, a = leaf // 2, leaf % 2
    y, b, c = grid // 4, (grid // 2) % 2, grid % 2
    front, idx = z // 2, leaf % 4
    same = a == b
    differ = jnp.logical_not(same)
    here_rows = pl.ds(pl.multiple_of(c * 256, 256), 256)

    def half_rows(h):
        return pl.ds(pl.multiple_of(c * 256 + h * 128, 128), 128)

    def at_idx(k):
        return (front * 4 + flip(idx, k), grid)

    def at_y(k):
        return (leaf, flip(y, k) * 4 + grid % 4)

    def at_z(k):
        return (flip(z, k) * 2 + a, grid)

    sibling = (leaf, grid + 1 - 2 * c)
    partner = (leaf, y * 4 + (1 - b) * 2 + c)
    def remote(src, dst, ss, rs, dev):
        return pltpu.make_async_remote_copy(
            src_ref=src, dst_ref=dst, send_sem=ss, recv_sem=rs, device_id=dev, device_id_type=MESH
        )

    bar = pltpu.get_barrier_semaphore()

    def greet(dev):
        pl.semaphore_signal(bar, inc=1, device_id=dev, device_id_type=MESH)

    @pl.loop(1, 16)
    def _(k):
        greet((leaf, (grid + k) % 16))

    greet(at_z(1))
    greet(at_z(3))
    for k in range(1, 4):
        x = (a * 2 + b + k) % 4
        greet(device(z, x // 2, y, x % 2, c))

    own_l = pltpu.make_async_copy(l_hbm, l_buf.at[0, here_rows], loc.at[4])
    own_l.start()

    def m_load(i):
        return pltpu.make_async_copy(m_hbm.at[pl.ds(i * 256, 256)], m_stage.at[i % 2], mst.at[i % 2])

    m_load(0).start()
    m_load(1).start()

    own_l.wait()
    for i in range(2):
        keep = pattern[leaf // 2, grid * 2 + i].astype(F32)
        l_buf[0, half_rows(i)] = l_buf[0, half_rows(i)] * keep

    pl.semaphore_wait(bar, 20)

    def own_s(h):
        return pltpu.make_async_copy(s_hbm.at[pl.ds(h * 128, 128)], s_buf.at[0, h, b], loc.at[h])

    def step(h, kind, n, dev):
        return remote(s_hbm.at[pl.ds(h * 128, 128)], s_buf.at[0, h, b], x_s.at[kind, h], x_r.at[n, h], dev)

    def step_one(h):
        return step(h, 0, 0, device(z, a, y, a, c))

    def step_two(h):
        return step(h, 1, 1, device(z, 1 - a, y, a, c))

    def step_out(h):
        return remote(s_hbm.at[pl.ds(h * 128, 128)], relay.at[h], x_s.at[0, h], x_r.at[1, h],
                      device(z, 1 - a, y, 1 - b, c))

    def step_on(h):
        return remote(relay.at[h], s_buf.at[0, h, 1 - b], x_s.at[1, h], x_r.at[0, h], device(z, a, y, 1 - b, c))

    def step_start(h):
        @pl.when(same)
        def _():
            own_s(h).start()
            step_out(h).start()

        @pl.when(differ)
        def _():
            step_one(h).start()
            step_two(h).start()

    def step_relay(h):
        @pl.when(same)
        def _():
            step_out(h).wait_recv()
            step_on(h).start()

    step_start(0)


    def y_own(src, buf, ss, rs, h, k):
        return remote(src, buf.at[k, half_rows(h)], ss.at[h, k], rs.at[h, k], at_y(k))

    def y_on(buf, ss, rs, h):
        came, way = (1, 3) if h == 0 else (3, 1)
        return remote(buf.at[came, half_rows(h)], buf.at[2, half_rows(h)], ss.at[h, 2], rs.at[h, 2], at_y(way))

    def p_own(h, k):
        return y_own(p_hbm.at[pl.ds(h * 128, 128)], p_col, py_s, py_r, h, k)

    def l_own(h, k):
        return y_own(l_buf.at[0, half_rows(h)], l_buf, ly_s, ly_r, h, k)

    for h, k in ((0, 1), (1, 3), (1, 1), (0, 3)):
        p_own(h, k).start()
    own_p = pltpu.make_async_copy(p_hbm, p_col.at[0, here_rows], loc.at[2])
    own_p.start()
    own_t = pltpu.make_async_copy(minv_hbm, t_row.at[0], loc.at[3])
    own_m = pltpu.make_async_copy(m_hbm.at[pl.ds(pl.multiple_of(grid * 128, 128), 128)], m_own, loc.at[5])
    own_t.start()
    own_m.start()

    def p_side(k):
        return remote(p_hbm if k == 0 else p_col.at[k, here_rows], p_col.at[k, here_rows],
                      ps_s.at[k], ps_r.at[k], sibling)

    def l_side(k):
        return remote(l_buf.at[k, here_rows], l_buf.at[k, here_rows], ls_s.at[k], ls_r.at[k], sibling)

    p_side(0).start()

    def split_m(i):
        m_load(i).wait()

        @pl.loop(0, 8)
        def _(n):
            rows = pl.ds(pl.multiple_of(n * 32, 32), 32)
            to = pl.ds(pl.multiple_of(i % 2 * 256 + n * 32, 32), 32)
            hi, lo = high_low(m_stage[i % 2, rows])
            m_hi[i // 2, to] = hi
            m_lo[i // 2, to] = lo
        if i + 2 < 8:
            m_load(i + 2).start()

    def split_rows(src, hi_ref, lo_ref, k):
        for n, m in enumerate((0, 2, 1, 3)):
            @pl.loop(0, 4)
            def _(i):
                rows = pl.ds(pl.multiple_of(m * 128 + i * 32, 32), 32)
                to = pl.ds(pl.multiple_of(n * 128 + i * 32, 32), 32)
                hi, lo = high_low(src[k, rows])
                hi_ref[k, to] = hi
                lo_ref[k, to] = lo

    def split_s(k, h):
        for bb in range(2):
            hi, lo = high_low(s_buf[k, h, bb])
            for part, base in ((hi, 0), (lo, 256)):
                at = slice(base + bb * 128, base + bb * 128 + 128)
                for n, m in enumerate((0, 2, 1, 3)):
                    s_split[k, h, at, n * 128:n * 128 + 128] = part[:, m * 128:m * 128 + 128]

    def accumulate(acc, lhs, rhs_hi, rhs_lo, first):
        m, n = acc.shape
        width = min(n, 512)

        @pl.loop(0, n // width)
        def _(j):
            cols = pl.ds(pl.multiple_of(j * width, width), width)
            hi = rhs_hi[:, cols]
            part = jnp.dot(lhs[0:m], hi, preferred_element_type=F32)
            part += jnp.dot(lhs[m:2 * m], hi, preferred_element_type=F32)
            part += jnp.dot(lhs[0:m], rhs_lo[:, cols], preferred_element_type=F32)
            if first:
                acc[:, cols] = part
            else:
                acc[:, cols] += part

    def z_own(h, bb, k):
        return remote(s_buf.at[0, h, bb], s_buf.at[k, h, bb], z_s.at[h, bb, k], z_r.at[h, bb, k], at_z(k))

    def z_on(h, bb):
        came, way = (1, 3) if bb == 0 else (3, 1)
        return remote(s_buf.at[came, h, bb], s_buf.at[2, h, bb], z_s.at[h, bb, 2], z_r.at[h, bb, 2], at_z(way))

    def s_here(h):
        @pl.when(same)
        def _():
            own_s(h).wait()
            step_one(h).wait_recv()

        @pl.when(differ)
        def _():
            step_one(h).wait_recv()
            step_two(h).wait_recv()
        for bb, k in ((0, 1), (1, 3), (1, 1), (0, 3)):
            z_own(h, bb, k).start()

    def s_on(h):
        z_own(h, 0, 1).wait_recv()
        z_on(h, 0).start()
        z_own(h, 1, 3).wait_recv()
        z_on(h, 1).start()

    def f_chunk(h, k, first=False):
        split_s(k, h)
        ky = either(y, flip(z, k))
        accumulate(f_part.at[h], s_split.at[k, h], p_hi.at[ky], p_lo.at[ky], first)

    def f_near(h):
        for k, bb in ((1, 1), (3, 0)):
            z_own(h, bb, k).wait_recv()
            f_chunk(h, k)

    other_rows = pl.ds(pl.multiple_of((1 - b) * 128, 128), 128)
    own_rows = pl.ds(pl.multiple_of(b * 128, 128), 128)

    def fx(h):
        return remote(f_part.at[h, other_rows], f_recv.at[h], fx_s.at[h], fx_r.at[h], partner)

    def f_last(h):
        z_on(h, 0).wait_recv()
        z_on(h, 1).wait_recv()
        f_chunk(h, 2)
        fx(h).start()

    def fr(k, h):
        src = frow.at[1, h] if k == 3 else frow.at[0, h]
        return remote(src, frow.at[k, h], fr_s.at[k, h], fr_r.at[k, h], at_idx(1 if k == 1 else 2))

    def f_final(h):
        fx(h).wait_recv()
        whole = f_part[h, own_rows] + f_recv[h]
        for cc in range(2):
            for bb in range(2):
                at = bb * 256 + cc * 128
                frow[0, h, cc, :, bb * 128:bb * 128 + 128] = whole[:, at:at + 128]
        fr(1, h).start()
        fr(2, h).start()
        f_out[h * 128:h * 128 + 128] = -whole

    def ft_far(k, h, cc):
        return remote(frow.at[k, h, cc], ft.at[y, c, h], ft_s.at[h, k, cc], ft_r.at[h, y, c],
                      (leaf, flip(idx, k) * 4 + b * 2 + cc))

    def ft_near(k, h):
        return pltpu.make_async_copy(frow.at[k, h, c], ft.at[y, c, h], loc.at[6 + h])

    def ft_send(k, h):
        for cc in range(2):
            mine = (flip(idx, k) == y) & (c == cc)

            @pl.when(mine)
            def _():
                ft_near(k, h).start()

            @pl.when(jnp.logical_not(mine))
            def _():
                ft_far(k, h, cc).start()

    def fr_step(k, h):
        fr(k, h).wait_recv()
        if k == 1:
            fr(3, h).start()
        ft_send(k, h)

    def root_chunk(h, ky, first=False):
        kz = either(z, flip(y, ky))
        accumulate(r_part.at[h], s_split.at[kz, h], l_hi.at[ky], l_lo.at[ky], first)

    def rx(h):
        return remote(r_part.at[h, other_rows], r_recv.at[h], rx_s.at[h], rx_r.at[h], partner)

    def l_ready(k):
        l_side(k).wait_recv()
        split_rows(l_buf, l_hi, l_lo, k)

    split_m(0)
    split_m(1)
    step_relay(0)
    step_start(1)
    split_m(2)
    p_own(0, 1).wait_recv()
    y_on(p_col, py_s, py_r, 0).start()
    p_own(1, 3).wait_recv()
    y_on(p_col, py_s, py_r, 1).start()
    for h, k in ((0, 1), (1, 3), (1, 1), (0, 3)):
        l_own(h, k).start()
    l_side(0).start()
    s_here(0)
    split_m(3)
    step_relay(1)
    p_own(1, 1).wait_recv()
    p_side(1).start()
    p_own(0, 3).wait_recv()
    p_side(3).start()
    split_m(4)
    s_on(0)
    s_here(1)
    split_m(5)
    own_p.wait()
    for k in (0, 1, 3):
        p_side(k).wait_recv()
        split_rows(p_col, p_hi, p_lo, k)
    y_on(p_col, py_s, py_r, 0).wait_recv()
    y_on(p_col, py_s, py_r, 1).wait_recv()
    p_side(2).start()
    split_m(6)
    l_ready(0)
    p_side(2).wait_recv()
    split_rows(p_col, p_hi, p_lo, 2)
    f_chunk(0, 0, True)
    s_on(1)
    f_near(0)
    split_m(7)
    f_last(0)
    f_chunk(1, 0, True)

    l_own(0, 1).wait_recv()
    y_on(l_buf, ly_s, ly_r, 0).start()
    l_own(1, 3).wait_recv()
    y_on(l_buf, ly_s, ly_r, 1).start()
    f_final(0)
    ft_send(0, 0)
    root_chunk(0, 0, True)
    for k, h in ((1, 1), (3, 0)):
        l_own(h, k).wait_recv()
        l_side(k).start()
    f_near(1)
    l_ready(1)
    root_chunk(0, 1)
    l_ready(3)
    f_last(1)
    fr_step(1, 0)
    fr_step(2, 0)
    root_chunk(0, 3)
    y_on(l_buf, ly_s, ly_r, 0).wait_recv()
    y_on(l_buf, ly_s, ly_r, 1).wait_recv()
    l_side(2).start()
    f_final(1)
    f_done = pltpu.make_async_copy(f_out, f_hbm, loc.at[8])
    f_done.start()
    ft_send(0, 1)
    l_ready(2)
    root_chunk(0, 2)
    rx(0).start()
    fr_step(3, 0)
    root_chunk(1, 0, True)
    fr_step(1, 1)
    fr_step(2, 1)
    for k in (1, 3):
        root_chunk(1, k)
    fr_step(3, 1)
    root_chunk(1, 2)
    rx(1).start()

    tx = remote(t_part.at[other_rows], t_recv, tx_s.at[0], tx_r.at[0], partner)

    def tr(k):
        return remote(t_row.at[1] if k == 3 else t_row.at[0], t_row.at[k], tr_s.at[k], tr_r.at[k],
                      at_idx(1 if k == 1 else 2))

    def t_chunk(h, k, first):
        far = flip(y, k)
        for cc in range(2):
            came = remote(frow.at[0, h, cc], ft.at[far, cc, h], ft_s.at[h, 0, cc], ft_r.at[h, far, cc], sibling)
            if k == 0:
                @pl.when(c == cc)
                def _():
                    ft_near(0, h).wait()

                @pl.when(c != cc)
                def _():
                    came.wait_recv()
            else:
                came.wait_recv()
            hi, lo = high_low(ft[far, cc, h].T)
            ft_split[k, 0:256, h * 256 + cc * 128:h * 256 + cc * 128 + 128] = hi
            ft_split[k, 256:512, h * 256 + cc * 128:h * 256 + cc * 128 + 128] = lo
        rows = slice(h * 256, h * 256 + 256)
        accumulate(t_part, ft_split.at[k, :, rows], p_hi.at[k, rows], p_lo.at[k, rows], first)

    for k in (0, 1, 3, 2):
        t_chunk(0, k, k == 0)

    for k in (0, 1, 3, 2):
        t_chunk(1, k, False)
    tx.start()
    for k in range(4):
        accumulate(q_part, ft_split.at[k], l_hi.at[k], l_lo.at[k], k == 0)
    own_t.wait()
    tx.wait_recv()
    t_row[0] = t_row[0] + (t_part[own_rows] + t_recv[...])
    tr(1).start()
    tr(2).start()
    qx = remote(q_part.at[other_rows], q_recv, qx_s.at[0], qx_r.at[0], partner)
    qx.start()

    for k in range(4):
        for h in range(2):
            for cc in range(2):
                hi, lo = high_low(frow[k, h, cc])
                for bb in range(2):
                    at = bb * 256 + cc * 128
                    part = slice(bb * 128, bb * 128 + 128)
                    a_tmp[h * 128:h * 128 + 128, at:at + 128] = hi[:, part]
                    a_tmp[256 + h * 128:256 + h * 128 + 128, at:at + 128] = lo[:, part]
        accumulate(fm, a_tmp, m_hi.at[flip(idx, k)], m_lo.at[flip(idx, k)], k == 0)
    row_at = grid * 128 + lax.broadcasted_iota(jnp.int32, (128, 512), 0)
    col_at = idx * 512 + lax.broadcasted_iota(jnp.int32, (128, 512), 1)
    mid = jnp.sum(jnp.where(row_at == col_at, t_row[0], 0.0), axis=0, keepdims=True)
    for i in range(4):
        sums[0, 8 + i:9 + i] = mid[:, i * 128:i * 128 + 128]
        sums[0, 12 + i:13 + i] = jnp.zeros((1, 128), F32)

    tr(1).wait_recv()
    tr(3).start()

    def root_done(h):
        return pltpu.make_async_copy(r_recv.at[h], root_hbm.at[pl.ds(h * 128, 128)], loc.at[9 + h])

    low = jnp.zeros((1, 1024), F32)
    for h in range(2):
        rx(h).wait_recv()
        rows = slice(h * 128, h * 128 + 128)
        root = r_part[h, own_rows] + r_recv[h] - fm[rows]
        r_recv[h] = -root
        root_done(h).start()
        low += jnp.sum(l_buf[0, half_rows(h)] * root, axis=0, keepdims=True)

    for k in range(4):
        if k > 1:
            tr(k).wait_recv()
        hi, lo = high_low(t_row[k])
        t_tmp[0:128] = hi
        t_tmp[128:256] = lo
        accumulate(tm, t_tmp, m_hi.at[flip(idx, k)], m_lo.at[flip(idx, k)], k == 0)

    own_m.wait()
    qx.wait_recv()
    par = tm[...] - (q_part[own_rows] + q_recv[...])
    q_recv[...] = -par
    par_done = pltpu.make_async_copy(q_recv, par_hbm, loc.at[11])
    par_done.start()
    low += jnp.sum(m_own[...] * par, axis=0, keepdims=True)
    for i in range(8):
        sums[0, i:i + 1] = low[:, i * 128:i * 128 + 128]

    def sum_copy(k):
        return remote(sums.at[0], sums.at[k], sum_s.at[k], sum_r.at[k], (leaf, (grid + k) % 16))

    for k in range(1, 16):
        sum_copy(k).start()
    total = sums[0]
    for k in range(1, 16):
        sum_copy(k).wait_recv()
    for k in range(1, 16):
        total += sums[k]
    sum_out[0:8] = total[0:8] + diag_ref[...]
    sum_out[8:16] = total[8:16]
    f_done.wait()
    for h in range(2):
        root_done(h).wait()
    par_done.wait()

    @pl.when(same)
    def _():
        for h in range(2):
            step_out(h).wait_send()
            step_on(h).wait_send()

    @pl.when(differ)
    def _():
        for h in range(2):
            step_one(h).wait_send()
            step_two(h).wait_send()
    for h in range(2):
        for k in (1, 3):
            p_own(h, k).wait_send()
            l_own(h, k).wait_send()
            for bb in range(2):
                z_own(h, bb, k).wait_send()
        y_on(p_col, py_s, py_r, h).wait_send()
        y_on(l_buf, ly_s, ly_r, h).wait_send()
        for bb in range(2):
            z_on(h, bb).wait_send()
    for k in range(4):
        p_side(k).wait_send()
        l_side(k).wait_send()
    for h in range(2):
        fx(h).wait_send()
        rx(h).wait_send()
        for k in range(4):
            if k:
                fr(k, h).wait_send()
            for cc in range(2):
                @pl.when(jnp.logical_not((flip(idx, k) == y) & (c == cc)))
                def _():
                    ft_far(k, h, cc).wait_send()
    tx.wait_send()
    for k in range(1, 4):
        tr(k).wait_send()
    qx.wait_send()
    for k in range(1, 16):
        sum_copy(k).wait_send()


def finish(first, root, par, total_hbm, first_out, mid_out, root_out, par_out, low_out, f_buf, r_buf, q_buf, total, sem):
    pairs = ((root, r_buf, root_out), (first, f_buf, first_out), (par, q_buf, par_out))
    come = [pltpu.make_async_copy(src, buf, sem.at[0, i]) for i, (src, buf, _) in enumerate(pairs)]
    go = [pltpu.make_async_copy(buf, dst, sem.at[1, i]) for i, (_, buf, dst) in enumerate(pairs)]
    sums = pltpu.make_async_copy(total_hbm, total, sem.at[0, 3])
    for copy in come:
        copy.start()
    sums.start()
    for i in range(3):
        come[i].wait()
        go[i].start()
    sums.wait()
    for i in range(8):
        low_out[i * 128:i * 128 + 128] = total[i]
    for i in range(4):
        mid_out[i * 128:i * 128 + 128] = total[8 + i]
    for copy in go:
        copy.wait()


def local(root_inverse, middle_inverse, middle_panel, lower_root, lower_middle, block_pattern, lower_diagonal):
    dma = pltpu.SemaphoreType.DMA
    vmem = pl.BlockSpec(memory_space=pltpu.VMEM)
    hbm = pl.BlockSpec(memory_space=pl.ANY)
    scratch = [
        pltpu.VMEM(shape, F32)
        for shape in (
            (4, 2, 2, 128, 512), (4, 512, 512), (4, 512, 1024), (4, 2, 2, 128, 256), (4, 2, 2, 128, 256),
            (2, 256, 512), (2, 128, 512), (2, 256, 1024), (2, 128, 1024), (256, 1024), (128, 1024),
            (256, 512), (128, 512), (4, 128, 512),
            (2, 256, 1024), (128, 1024), (128, 1024), (256, 1024), (16, 16, 128), (2, 128, 512),
            (256, 512),
        )
    ] + [
        pltpu.VMEM(shape, BF16)
        for shape in (
            (4, 2, 512, 512), (4, 512, 1024), (4, 512, 1024), (4, 512, 1024), (4, 512, 1024),
            (4, 512, 512), (4, 512, 512), (512, 512), (256, 512), (4, 512, 512),
        )
    ] + [
        dma(shape)
        for shape in (
            (12,), (2,), (2, 2), (2, 2), (2, 2, 4), (2, 2, 4), (2, 4), (2, 4), (4,), (4,), (2, 4), (2, 4), (4,), (4,),
            (2,), (2,), (4, 2), (4, 2), (2, 4, 2), (2, 4, 2), (2,), (2,), (1,), (1,), (1,), (1,), (4,), (4,),
            (16,), (16,),
        )
    ]
    blocks = tuple(jax.ShapeDtypeStruct(shape, F32) for shape in ((256, 512), (256, 1024), (128, 1024)))
    first, root, par, total = pl.pallas_call(
        kernel,
        out_shape=blocks + (jax.ShapeDtypeStruct((16, 128), F32),),
        in_specs=[hbm, hbm, hbm, hbm, hbm, pl.BlockSpec(memory_space=pltpu.SMEM), vmem],
        out_specs=(hbm, hbm, hbm, vmem),
        scratch_shapes=scratch,
        compiler_params=pltpu.CompilerParams(
            collective_id=0, has_side_effects=True, vmem_limit_bytes=62 * MIB
        ),
        cost_estimate=pl.CostEstimate(flops=20 * 10**9, bytes_accessed=16 * MIB, transcendentals=0),
        name="selected_inverse",
    )(
        root_inverse, middle_inverse, middle_panel, lower_root, lower_middle, block_pattern,
        lower_diagonal.reshape(8, 128),
    )
    return pl.pallas_call(
        finish,
        out_shape=(
            blocks[0], jax.ShapeDtypeStruct((512,), F32), blocks[1], blocks[2], jax.ShapeDtypeStruct((1024,), F32),
        ),
        in_specs=[hbm, hbm, hbm, hbm],
        out_specs=(hbm, vmem, hbm, hbm, vmem),
        scratch_shapes=[pltpu.VMEM(x.shape, F32) for x in (first, root, par, total)] + [dma((2, 4))],
        compiler_params=pltpu.CompilerParams(vmem_limit_bytes=62 * MIB),
        name="hand_over",
    )(first, root, par, total)


def solution(mesh):
    in_specs = (
        P("grid", "leaf"),
        P("grid", "leaf"),
        P("grid", "leaf"),
        P("grid", "leaf"),
        P(None, "leaf"),
        P(),
        P("leaf"),
    )
    out_specs = (P("grid", "leaf"), P("leaf"), P("grid", "leaf"), P("grid", "leaf"), P("leaf"))
    return jax.shard_map(local, mesh=mesh, in_specs=in_specs, out_specs=out_specs, check_vma=False)
```
